512 devices in a mesh: dp: 8 (over x, core), expert: 64 (over z, y).
Axes of the slice: x: 4, y: 4, z: 16, core: 2. Of those that a mesh axis runs over, the one named last changes fastest.
Arguments:
- tokens: bfloat16 [65536, 512], P(('dp', 'expert')), may hold values from -6 to 6
- expert_ids: int32 [65536, 8], P(('dp', 'expert')), may hold values from 0 to 63, all different within a row; in each aligned block of 128 rows (0 to 127, 128 to 255, ...) at most 20 rows name the same one
- gate_weights: float32 [65536, 8], P(('dp', 'expert')), may hold values from 0.1 to 1
- cotangent: bfloat16 [65536, 512], P(('dp', 'expert')), may hold values from -6 to 6
- w_gate: bfloat16 [64, 512, 512], P('expert'), may hold values from -0.25 to 0.25
- w_up: bfloat16 [64, 512, 512], P('expert'), may hold values from -0.25 to 0.25
- w_down: bfloat16 [64, 512, 512], P('expert'), may hold values from -0.25 to 0.25
Outputs:
- layer_out: bfloat16 [65536, 512], P(('dp', 'expert'))
- grad_tokens: bfloat16 [65536, 512], P(('dp', 'expert'))
- grad_gates: float32 [65536, 8], P(('dp', 'expert'))
- grad_w_gate: bfloat16 [64, 512, 512], P('expert')
- grad_w_up: bfloat16 [64, 512, 512], P('expert')
- grad_w_down: bfloat16 [64, 512, 512], P('expert')
The draws below stay inside these ranges and needn't reach their ends.
Inputs may be any that keep to these rules, and one draw needn't show every extreme that they name: `expert_ids`: each row names 8 different experts. Among the 128 rows of one device no expert is named by more than 20 rows, a bound that some block reaches.
All inputs are finite; a program needn't handle non-finite values.
Results may differ from the reference program's by a relative error of at most 0.0064.
Values may be sent and summed in bfloat16 or wider, within the bound.
No kernel may reach another device: no remote copies, remote signals or barrier semaphores. Data moves between devices by JAX's collectives and lax.ppermute only.
A program may use at most 64 MiB of HBM per device.

```python
import math
import jax
import jax.numpy as jnp
import numpy as np
from jax import lax

L = 512
H = 512
TOP = 8
TOK_DEV = 128
EXPERTS = 64
TOKENS = 65536
CAP = 20
ROWS_EXPERT = 8192
N_DP = 8
N_EXPERT = 64


def shard_levels(key, dims, split, low, top_value):
    def one(dim, blocks):
        steps = jax.random.uniform(jax.random.fold_in(jax.random.fold_in(key, 6), dim), (blocks,), jnp.float32, low / len(split), top_value / len(split))
        return jnp.repeat(jnp.exp(steps), dims[dim] // blocks).reshape((-1,) + (1,) * (len(dims) - dim - 1))

    gain = one(*split[0])
    for cut in split[1:]:
        gain = gain * one(*cut)
    return gain


def assign_block(rng, own, number, rows, amount, top, bound, lean):
    ranking = jax.random.permutation(rng, amount)
    packed, ordinary = shares(amount, rows * top, bound, lean, True), shares(amount, rows * top, bound, lean, False)
    places = jnp.arange(amount)

    def named(sizes, rotation):
        used = int((sizes > 0).sum())
        fixed = max(1, used // 4)
        moved = fixed + (places - fixed + rotation * (used - fixed)) % max(1, amount - fixed)
        return jnp.zeros((amount,), jnp.int32).at[ranking[jnp.where(places < fixed, places, moved)]].set(jnp.asarray(sizes, jnp.int32))

    sizes = jnp.where(number % 4 == 0, named(packed, number // 4), named(ordinary, number - number // 4 - 1))
    mixed = jax.random.permutation(jax.random.fold_in(own, 3), amount)
    giver, receiver = mixed[0:amount // 2 * 2:2], mixed[1:amount // 2 * 2:2]
    room = jnp.minimum(sizes[giver] - 1, bound - sizes[receiver]) // 2
    room = jnp.where((giver == ranking[0]) | (receiver == ranking[0]) | (sizes[receiver] == 0), 0, jnp.maximum(room, 0))
    moved = jax.random.randint(jax.random.fold_in(own, 4), (amount // 2,), 0, 1 << 20) % (room + 1)
    sizes = sizes.at[giver].add(-moved).at[receiver].add(moved)
    labels = jnp.searchsorted(jnp.cumsum(sizes), jnp.arange(rows * top), side="right").astype(jnp.int32)
    listing = labels.reshape(top, rows).T
    listing = listing[jax.random.permutation(jax.random.fold_in(own, 1), rows)]
    rotation = jax.random.randint(jax.random.fold_in(own, 2), (rows, 1), 0, top)
    return jnp.take_along_axis(listing, (jnp.arange(top)[None, :] + rotation) % top, axis=1)


def shares(number_of, total, bound, skew, full):
    loads = [(1 << 20) // math.isqrt(grade ** skew) + 1 for grade in range(1, number_of + 1)]
    largest = bound if full else min(bound, max(-(-total // number_of), total * loads[0] // sum(loads)))
    least = 1 if total - largest >= number_of - 1 else 0
    given, spare = [largest] + [least] * (number_of - 1), total - largest - least * (number_of - 1)
    while spare > 0:
        movable = [i for i in range(1, number_of) if given[i] < largest] or [i for i in range(1, number_of) if given[i] < bound]
        mass, remaining = sum([loads[i] for i in movable]), spare
        for i in movable:
            addition = min(bound - given[i], max(1, remaining * loads[i] // mass), spare)
            given[i] = given[i] + addition
            spare = spare - addition
    return np.array(given)


def centred(own_key, extent, deviation, most, pieces=(), kind=jnp.bfloat16):
    entries = jax.random.normal(own_key, extent, jnp.float32) * deviation
    if len(pieces) > 0:
        entries = shard_levels(own_key, extent, pieces, -0.22, 0.18) * entries
    return jnp.clip(entries, min=-most, max=most).astype(kind)


def setup_inputs(seed: int = 0) -> dict:
    streams_of = jax.random.split(jax.random.key(seed), 8)
    tokens = centred(streams_of[0], (TOKENS, L), 1.0, 6.0, ((0, 512),))
    expert_ids_keys = jax.random.split(jax.random.fold_in(streams_of[1], 1), TOKENS // TOK_DEV)
    expert_ids_turns = jax.random.permutation(jax.random.fold_in(streams_of[1], 3), TOKENS // TOK_DEV)
    expert_ids = jax.vmap(lambda own, number: assign_block(jax.random.fold_in(streams_of[1], 2), own, number, TOK_DEV, EXPERTS, TOP, CAP, 2))(expert_ids_keys, expert_ids_turns).reshape((TOKENS, TOP))
    gate_weights = jnp.clip(jnp.exp(math.log(1.0) - 2.3025851 * jax.random.uniform(streams_of[2], (TOKENS, TOP), jnp.float32) ** shard_levels(streams_of[2], (TOKENS, TOP), ((0, 512),), -0.2, 0.2)), 0.1, 1.0)
    cotangent = centred(streams_of[3], (TOKENS, L), 1.0, 6.0, ((0, 512),))
    w_gate = centred(streams_of[4], (EXPERTS, L, H), L ** -0.5, 0.25, ((0, 64),))
    w_up = centred(streams_of[5], (EXPERTS, L, H), L ** -0.5, 0.25, ((0, 64),))
    w_down = centred(streams_of[6], (EXPERTS, H, L), H ** -0.5, 0.25, ((0, 64),))
    return dict(tokens=tokens, expert_ids=expert_ids, gate_weights=gate_weights, cotangent=cotangent, w_gate=w_gate, w_up=w_up, w_down=w_down)


def silu_parts(pre_act):
    sigmoid_val = jax.nn.sigmoid(pre_act)
    return pre_act * sigmoid_val, sigmoid_val * (1.0 + pre_act * (1.0 - sigmoid_val))


def reference(tokens, expert_ids, gate_weights, cotangent, w_gate, w_up, w_down):
    device_count = N_DP * N_EXPERT
    assign_count = TOK_DEV * TOP
    row_count = device_count * CAP
    assign_total = TOKENS * TOP
    flat_ids = expert_ids.reshape(device_count, assign_count)
    onehot = (flat_ids[:, :, None] == jnp.arange(EXPERTS, dtype=jnp.int32)[None, None, :]).astype(jnp.int32)
    slot_index = jnp.sum((jnp.cumsum(onehot, axis=1) - onehot) * onehot, axis=2).astype(jnp.int32)
    devices = jnp.arange(device_count, dtype=jnp.int32)[:, None]
    assign = (devices * assign_count + jnp.arange(assign_count, dtype=jnp.int32)[None, :]).astype(jnp.int32)
    slot_table = jnp.full((EXPERTS, row_count), assign_total, jnp.int32)
    slot_table = slot_table.at[flat_ids, (devices * CAP + slot_index).astype(jnp.int32)].set(assign)
    tok_pad = jnp.concatenate([tokens, jnp.zeros((1, L), tokens.dtype)], 0)
    cot_pad = jnp.concatenate([cotangent, jnp.zeros((1, L), cotangent.dtype)], 0)
    gate_pad = jnp.concatenate([gate_weights.reshape(-1), jnp.zeros((1,), gate_weights.dtype)], 0)

    def per_expert(carry, inputs):
        mixed_sum, token_grad, gate_grad = carry
        row_ids, gate_mat, up_mat, down_mat = inputs
        token_ids = (row_ids // TOP).astype(jnp.int32)
        rows_in = tok_pad[token_ids]
        weight = gate_pad[row_ids]
        gate_pre = jnp.dot(rows_in, gate_mat, preferred_element_type=jnp.float32)
        up_pre = jnp.dot(rows_in, up_mat, preferred_element_type=jnp.float32)
        activation, derivative = silu_parts(gate_pre)
        hidden = (activation * up_pre).astype(jnp.bfloat16)
        expert_out = jnp.dot(hidden, down_mat, preferred_element_type=jnp.float32).astype(jnp.bfloat16)
        out_wide = expert_out.astype(jnp.float32)
        cot_rows = cot_pad[token_ids].astype(jnp.float32)
        out_grad = (weight[:, None] * cot_rows).astype(jnp.bfloat16)
        hidden_grad = jnp.dot(out_grad, down_mat.T, preferred_element_type=jnp.float32)
        gate_back = (hidden_grad * up_pre * derivative).astype(jnp.bfloat16)
        up_back = (hidden_grad * activation).astype(jnp.bfloat16)
        input_back = (jnp.dot(gate_back, gate_mat.T, preferred_element_type=jnp.float32)
                      + jnp.dot(up_back, up_mat.T, preferred_element_type=jnp.float32)).astype(jnp.bfloat16)
        mixed_sum = mixed_sum.at[token_ids].add(weight[:, None] * out_wide)
        token_grad = token_grad.at[token_ids].add(input_back.astype(jnp.float32))
        gate_grad = gate_grad.at[row_ids].set(jnp.sum(cot_rows * out_wide, axis=1))
        weight_grads = (jnp.dot(rows_in.T, gate_back, preferred_element_type=jnp.float32),
                        jnp.dot(rows_in.T, up_back, preferred_element_type=jnp.float32),
                        jnp.dot(hidden.T, out_grad, preferred_element_type=jnp.float32))
        return (mixed_sum, token_grad, gate_grad), weight_grads

    start = (jnp.zeros((TOKENS + 1, L), jnp.float32), jnp.zeros((TOKENS + 1, L), jnp.float32),
             jnp.zeros((assign_total + 1,), jnp.float32))
    carry, weight_grads = lax.scan(per_expert, start, (slot_table, w_gate, w_up, w_down))
    grad_scale = float(ROWS_EXPERT) ** -0.5
    return (carry[0][:TOKENS].astype(jnp.bfloat16),
            carry[1][:TOKENS].astype(jnp.bfloat16),
            carry[2][:assign_total].reshape(TOKENS, TOP),
            (weight_grads[0] * grad_scale).astype(jnp.bfloat16),
            (weight_grads[1] * grad_scale).astype(jnp.bfloat16),
            (weight_grads[2] * grad_scale).astype(jnp.bfloat16))
```

```python
import functools
import jax
import jax.numpy as jnp
from jax import lax
from jax.experimental import pallas as pl
from jax.experimental.pallas import tpu as pltpu
from jax.sharding import Mesh, PartitionSpec as P

BF = jnp.bfloat16
F32 = jnp.float32
TOK = 128
WIDTH = 512
TOP = 8
CAP = 20
HI = 8
LO = 8
PACK = 4
GROUPS = HI // PACK
SLOTS = PACK * CAP
GTOK = PACK * TOK
LANES = 128
CUTS = WIDTH // LANES
SENT = 2 * WIDTH + 4 * TOP
BACK = 2 * WIDTH + 2 * TOP
ROWS = HI * CAP * LO
PARAMS = pltpu.CompilerParams(vmem_limit_bytes=56 * 1024 * 1024)
VMEM = pl.BlockSpec(memory_space=pltpu.VMEM)
SMEM = pl.BlockSpec(memory_space=pltpu.SMEM)


def nn(a, b):
    return jnp.dot(a, b, preferred_element_type=F32)


def nt(a, b):
    return lax.dot_general(a, b, (((1,), (1,)), ((), ())), preferred_element_type=F32)


def tn(a, b):
    return lax.dot_general(a, b, (((0,), (0,)), ((), ())), preferred_element_type=F32)


def call(kernel, shapes, args, scratch=(), scalars=0, flops=0):
    moved = sum(a.size * a.dtype.itemsize for a in args)
    moved += sum(s.size * s.dtype.itemsize for s in shapes)
    return pl.pallas_call(
        kernel,
        out_shape=shapes,
        in_specs=[SMEM] * scalars + [VMEM] * (len(args) - scalars),
        out_specs=[VMEM] * len(shapes),
        scratch_shapes=list(scratch),
        compiler_params=PARAMS,
        cost_estimate=pl.CostEstimate(flops=flops, bytes_accessed=moved, transcendentals=0),
    )(*args)


def pack_kernel(tok, ids, gates, cot, out):
    for f in range(CUTS):
        cut = slice(f * LANES, (f + 1) * LANES)
        out[f * TOK : (f + 1) * TOK, :] = tok[:, cut]
        out[WIDTH + f * TOK : WIDTH + (f + 1) * TOK, :] = cot[:, cut]
    gate = gates[...]
    high = gate.astype(BF).astype(F32)
    middle = (gate - high).astype(BF).astype(F32)
    low = gate - high - middle
    at = 2 * WIDTH
    out[at : at + 16, :] = jnp.concatenate([ids[...].astype(F32), high], axis=0).astype(BF)
    out[at + 16 : at + 32, :] = jnp.concatenate([middle, low], axis=0).astype(BF)


def group_rows(ref, group, first, count):
    parts = []
    for b in range(PACK):
        at = (group * PACK + b) * SENT + first
        parts.append(ref[at : at + count, :].astype(F32))
    return jnp.concatenate(parts, axis=1)


def dispatch_kernel(first, got, x_out, og_out, rank_out, gate_out, tok_s, cot_s):
    base = (first[0] * LO).astype(F32)
    row = lax.broadcasted_iota(jnp.int32, (GTOK, GTOK), 0)
    col = lax.broadcasted_iota(jnp.int32, (GTOK, GTOK), 1)
    upto = (row <= col).astype(F32).astype(BF)
    place = (lax.broadcasted_iota(jnp.int32, (SLOTS, GTOK), 0) + 1).astype(F32)
    for g in range(GROUPS):
        for b in range(PACK):
            at = (g * PACK + b) * SENT
            for f in range(CUTS):
                cut = slice(f * LANES, (f + 1) * LANES)
                rows = slice(b * TOK, (b + 1) * TOK)
                tok_s[rows, cut] = got[at + f * TOK : at + (f + 1) * TOK, :]
                cot_s[rows, cut] = got[at + WIDTH + f * TOK : at + WIDTH + (f + 1) * TOK, :]
        ids_high = group_rows(got, g, 2 * WIDTH, 16)
        middle_low = group_rows(got, g, 2 * WIDTH + 16, 16)
        ids = ids_high[:TOP]
        gates = (ids_high[TOP:] + middle_low[:TOP]) + middle_low[TOP:]
        named, weight = [], []
        for e in range(LO):
            same = ids == base + e
            named.append(jnp.sum(jnp.where(same, 1.0, 0.0), axis=0, keepdims=True))
            weight.append(jnp.sum(jnp.where(same, gates, 0.0), axis=0, keepdims=True))
        named = jnp.concatenate(named, axis=0)
        rank_out[g * LO : (g + 1) * LO, :] = named * nn(named.astype(BF), upto)
        gate_out[g * LO : (g + 1) * LO, :] = jnp.concatenate(weight, axis=0)

        def one(e, carry):
            picks = rank_out[pl.ds(g * LO + e, 1), :] == place
            picked = jnp.where(picks, 1.0, 0.0).astype(BF)
            to = pl.ds(pl.multiple_of((e * GROUPS + g) * SLOTS, 16), SLOTS)
            x_out[to, :] = nn(picked, tok_s[...]).astype(BF)
            gate = jnp.where(picks, gate_out[pl.ds(g * LO + e, 1), :], 0.0)
            og_out[to, :] = (
                jnp.sum(gate, axis=1, keepdims=True) * nn(picked, cot_s[...])
            ).astype(BF)
            return carry

        lax.fori_loop(0, LO, one, 0)


TILE = 160


def forward_kernel(x, w_gate, w_up, w_down, out, hidden, act, slope):
    def one(i, carry):
        rows = pl.ds(pl.multiple_of(i * TILE, 16), TILE)
        gate_pre = nn(x[rows, :], w_gate[...])
        up_pre = nn(x[rows, :], w_up[...])
        sig = jax.nn.sigmoid(gate_pre)
        activation = gate_pre * sig
        mixed = (activation * up_pre).astype(BF)
        hidden[rows, :] = mixed
        act[rows, :] = activation
        slope[rows, :] = up_pre * (sig * (1.0 + gate_pre * (1.0 - sig)))
        out[rows, :] = nn(mixed, w_down[...]).astype(BF)
        return carry

    lax.fori_loop(0, ROWS // TILE, one, 0)


def backward_kernel(og, act, slope, w_gate, w_up, w_down, out, gate_back, up_back):
    def one(i, carry):
        rows = pl.ds(pl.multiple_of(i * TILE, 16), TILE)
        hidden_grad = nt(og[rows, :], w_down[...])
        gate = (hidden_grad * slope[rows, :]).astype(BF)
        up = (hidden_grad * act[rows, :]).astype(BF)
        gate_back[rows, :] = gate
        up_back[rows, :] = up
        out[rows, :] = (nt(gate, w_gate[...]) + nt(up, w_up[...])).astype(BF)
        return carry

    lax.fori_loop(0, ROWS // TILE, one, 0)


def weight_kernel(x, og, hidden, gate_back, up_back, out):
    out[0:WIDTH, :] = tn(x[...], gate_back[...]).astype(BF)
    out[WIDTH : 2 * WIDTH, :] = tn(x[...], up_back[...]).astype(BF)
    out[2 * WIDTH : 3 * WIDTH, :] = tn(hidden[...], og[...]).astype(BF)


def split(value):
    high = value.astype(BF)
    return high, (value - high.astype(F32)).astype(BF)


def combine_kernel(first, got, rank, gate, eo, ib, out, cot_s, eo_s, ib_s):
    base = (first[0] * LO).astype(F32)
    slots = LO * SLOTS
    expert = lax.broadcasted_iota(jnp.int32, (LO, slots), 0)
    slot = lax.broadcasted_iota(jnp.int32, (LO, slots), 1)
    spread = ((slot >= expert * SLOTS) & (slot < (expert + 1) * SLOTS)).astype(F32).astype(BF)
    lane = lax.broadcasted_iota(jnp.int32, (1, slots), 1)
    place = (lane - SLOTS * lax.div(lane, SLOTS) + 1).astype(F32)
    for g in range(GROUPS):
        for b in range(PACK):
            at = (g * PACK + b) * SENT + WIDTH
            for f in range(CUTS):
                cot_s[b * TOK : (b + 1) * TOK, f * LANES : (f + 1) * LANES] = got[
                    at + f * TOK : at + (f + 1) * TOK, :
                ]
        for e in range(LO):
            at = (e * GROUPS + g) * SLOTS
            eo_s[e * SLOTS : (e + 1) * SLOTS, :] = eo[at : at + SLOTS, :]
            ib_s[e * SLOTS : (e + 1) * SLOTS, :] = ib[at : at + SLOTS, :]
        rows = slice(g * LO, (g + 1) * LO)
        ranks = tn(rank[rows, :].astype(BF), spread)
        picks = ranks == place
        high, low = split(gate[rows, :])
        high = jnp.where(picks, tn(high, spread), 0.0).astype(BF)
        low = jnp.where(picks, tn(low, spread), 0.0).astype(BF)
        layer = nn(high, eo_s[...]) + nn(low, eo_s[...])
        back = nn(jnp.where(picks, 1.0, 0.0).astype(BF), ib_s[...])
        along = jnp.where(picks, nt(cot_s[...], eo_s[...]), 0.0)
        high, low = split(along)
        along = nt(spread, high) + nt(spread, low)
        ids = group_rows(got, g, 2 * WIDTH, 16)[:TOP]
        grad = jnp.zeros((TOP, GTOK), F32)
        for e in range(LO):
            grad += jnp.where(ids == base + e, along[e : e + 1, :], 0.0)
        grad_high = grad.astype(BF).astype(F32)
        grad = jnp.concatenate([grad_high, grad - grad_high], axis=0).astype(BF)
        for b in range(PACK):
            at = (g * PACK + b) * BACK
            for f in range(CUTS):
                here = (slice(b * TOK, (b + 1) * TOK), slice(f * LANES, (f + 1) * LANES))
                out[at + f * TOK : at + (f + 1) * TOK, :] = layer[here].astype(BF)
                out[at + WIDTH + f * TOK : at + WIDTH + (f + 1) * TOK, :] = back[here].astype(BF)
            out[at + 2 * WIDTH : at + BACK, :] = grad[:, b * TOK : (b + 1) * TOK]


def unpack_kernel(got, layer, back, grad):
    for f in range(CUTS):
        cut = slice(f * LANES, (f + 1) * LANES)
        layer[:, cut] = got[f * TOK : (f + 1) * TOK, :]
        back[:, cut] = got[WIDTH + f * TOK : WIDTH + (f + 1) * TOK, :]
    parts = got[2 * WIDTH : BACK, :].astype(F32)
    grad[...] = parts[:TOP] + parts[TOP:]


def body(tokens, expert_ids, gate_weights, cotangent, w_gate, w_up, w_down):
    shape = jax.ShapeDtypeStruct
    first = lax.axis_index("hi").astype(jnp.int32).reshape(1)
    w_gate, w_up, w_down = w_gate[0], w_up[0], w_down[0]
    square = 2 * ROWS * WIDTH * WIDTH
    (packed,) = call(
        pack_kernel,
        [shape((SENT, LANES), BF)],
        [tokens, expert_ids.T, gate_weights.T, cotangent],
    )
    got = lax.all_gather(packed, "hi", axis=0, tiled=True)
    rows_in, out_grad, rank, gate = call(
        dispatch_kernel,
        [
            shape((ROWS, WIDTH), BF),
            shape((ROWS, WIDTH), BF),
            shape((GROUPS * LO, GTOK), F32),
            shape((GROUPS * LO, GTOK), F32),
        ],
        [first, got],
        [pltpu.VMEM((GTOK, WIDTH), BF), pltpu.VMEM((GTOK, WIDTH), BF)],
        scalars=1,
        flops=2 * square,
    )
    exchange = functools.partial(
        lax.all_to_all, axis_name="lo", split_axis=0, concat_axis=0, tiled=True
    )
    x = exchange(rows_in)
    og = exchange(out_grad)
    wide = shape((ROWS, WIDTH), F32)
    narrow = shape((ROWS, WIDTH), BF)
    expert_out, hidden, act, slope = call(
        forward_kernel,
        [narrow, narrow, wide, wide],
        [x, w_gate, w_up, w_down],
        flops=3 * square,
    )
    eo = exchange(expert_out)
    input_back, gate_back, up_back = call(
        backward_kernel,
        [narrow, narrow, narrow],
        [og, act, slope, w_gate, w_up, w_down],
        flops=3 * square,
    )
    ib = exchange(input_back)
    (weight_part,) = call(
        weight_kernel,
        [shape((3 * WIDTH, WIDTH), BF)],
        [x, og, hidden, gate_back, up_back],
        flops=3 * square,
    )
    (partial,) = call(
        combine_kernel,
        [shape((HI * BACK, LANES), BF)],
        [first, got, rank, gate, eo, ib],
        [
            pltpu.VMEM((GTOK, WIDTH), BF),
            pltpu.VMEM((LO * SLOTS, WIDTH), BF),
            pltpu.VMEM((LO * SLOTS, WIDTH), BF),
        ],
        scalars=1,
        flops=4 * square,
    )
    summed = lax.psum_scatter(partial, "hi", scatter_dimension=0, tiled=True)
    over_dp = functools.partial(
        lax.all_to_all, axis_name="dp", split_axis=0, concat_axis=0, tiled=True
    )
    data = lax.axis_size("dp")
    share = over_dp(weight_part).reshape(data, -1, WIDTH).astype(F32)
    grad_scale = float(data * TOK * TOP) ** (-0.5)
    share = (jnp.sum(share, axis=0) * grad_scale).astype(BF)
    weight_grad = over_dp(jnp.tile(share, (data, 1))).reshape(3, 1, WIDTH, WIDTH)
    layer_out, grad_tokens, grad_gates = call(
        unpack_kernel,
        [shape((TOK, WIDTH), BF), shape((TOK, WIDTH), BF), shape((TOP, LANES), F32)],
        [summed],
    )
    return (
        layer_out,
        grad_tokens,
        grad_gates.T,
        weight_grad[0],
        weight_grad[1],
        weight_grad[2],
    )


def solution(mesh):
    data = mesh.shape["dp"]
    cut = Mesh(mesh.devices.reshape(data, HI, LO), ("dp", "hi", "lo"))
    rows = P(("dp", "hi", "lo"), None)
    weight = P(("hi", "lo"), None, None)
    return jax.shard_map(
        body,
        mesh=cut,
        in_specs=(rows, rows, rows, rows, weight, weight, weight),
        out_specs=(rows, rows, rows, weight, weight, weight),
        check_vma=False,
    )
```

```python
import functools
import jax
import jax.numpy as jnp
from jax import lax
from jax.experimental import pallas as pl
from jax.experimental.pallas import tpu as pltpu
from jax.sharding import Mesh, PartitionSpec as P

BF = jnp.bfloat16
F32 = jnp.float32
TOK = 128
WIDTH = 512
TOP = 8
CAP = 20
HI = 8
LO = 8
PACK = 4
GROUPS = HI // PACK
SLOTS = PACK * CAP
GTOK = PACK * TOK
LANES = 128
CUTS = WIDTH // LANES
FIRST = 3
SECOND = CUTS - FIRST
LEAD = FIRST * LANES
TAIL = SECOND * LANES
SENT_RING = LEAD + 2 * TOP
SENT_REST = TAIL + WIDTH + 4 * TOP
AT_COT = TAIL
AT_GATES = TAIL + WIDTH
BACK = 2 * WIDTH + 2 * TOP
STEPS = [0] + [s for h in range(1, HI // 2) for s in (-h, h)] + [-(HI // 2)]
ALL = LO * SLOTS
ROWS = HI * CAP * LO
MIB = 1024 * 1024
VMEM = pl.BlockSpec(memory_space=pltpu.VMEM)
SMEM = pl.BlockSpec(memory_space=pltpu.SMEM)


def nn(a, b):
    return jnp.dot(a, b, preferred_element_type=F32)


def nt(a, b):
    return lax.dot_general(a, b, (((1,), (1,)), ((), ())), preferred_element_type=F32)


def tn(a, b):
    return lax.dot_general(a, b, (((0,), (0,)), ((), ())), preferred_element_type=F32)


def call(kernel, shapes, args, scratch=(), scalars=0, flops=0, room=24):
    moved = sum(a.size * a.dtype.itemsize for a in args)
    moved += sum(s.size * s.dtype.itemsize for s in shapes)
    return pl.pallas_call(
        kernel,
        out_shape=shapes,
        in_specs=[SMEM] * scalars + [VMEM] * (len(args) - scalars),
        out_specs=[VMEM] * len(shapes),
        scratch_shapes=list(scratch),
        compiler_params=pltpu.CompilerParams(vmem_limit_bytes=room * MIB),
        cost_estimate=pl.CostEstimate(flops=flops, bytes_accessed=moved, transcendentals=0),
    )(*args)


def pack_kernel(tok, ids, gates, cot, ring_out, rest_out):
    for f in range(CUTS):
        cut = slice(f * LANES, (f + 1) * LANES)
        to, at = (ring_out, f) if f < FIRST else (rest_out, f - FIRST)
        to[at * TOK : (at + 1) * TOK, :] = tok[:, cut]
        rest_out[AT_COT + f * TOK : AT_COT + (f + 1) * TOK, :] = cot[:, cut]
    gate = gates[...]
    high = gate.astype(BF).astype(F32)
    middle = (gate - high).astype(BF).astype(F32)
    low = gate - high - middle
    named = ids[...].astype(F32)
    ring_out[LEAD : LEAD + 16, :] = jnp.concatenate([named, named], axis=0).astype(BF)
    rest_out[AT_GATES : AT_GATES + 16, :] = jnp.concatenate([high, middle], axis=0).astype(BF)
    rest_out[AT_GATES + 16 : AT_GATES + 32, :] = jnp.concatenate([low, low], axis=0).astype(BF)


def upper(size):
    row = lax.broadcasted_iota(jnp.int32, (size, size), 0)
    col = lax.broadcasted_iota(jnp.int32, (size, size), 1)
    return (row <= col).astype(F32).astype(BF)


def place_rows():
    return (lax.broadcasted_iota(jnp.int32, (SLOTS, GTOK), 0) + 1).astype(F32)


def pick_rows(rank, group, pick_s):
    place = place_rows()
    for e in range(LO):
        picks = rank[group * LO + e : group * LO + e + 1, :] == place
        pick_s[e * SLOTS : (e + 1) * SLOTS, :] = jnp.where(picks, 1.0, 0.0).astype(BF)


def put_rows(out, group, rows, lanes):
    for e in range(LO):
        to = (e * GROUPS + group) * SLOTS
        out[to : to + SLOTS, lanes] = rows[e * SLOTS : (e + 1) * SLOTS, :].astype(BF)


def first_kernel(first, *refs):
    blocks, (x_out, rank_out, ids_out, tok_s, pick_s) = refs[:HI], refs[HI:]
    base = (first[0] * LO).astype(F32)
    upto = upper(GTOK)
    for g in range(GROUPS):
        part = []
        for b in range(PACK):
            got = blocks[g * PACK + b]
            for f in range(FIRST):
                cut = slice(f * LANES, (f + 1) * LANES)
                tok_s[b * TOK : (b + 1) * TOK, cut] = got[f * TOK : (f + 1) * TOK, :]
            part.append(got[LEAD : LEAD + 16, :].astype(F32)[:TOP])
        ids = jnp.concatenate(part, axis=1)
        ids_out[g * TOP : (g + 1) * TOP, :] = ids
        named = [
            jnp.sum(jnp.where(ids == base + e, 1.0, 0.0), axis=0, keepdims=True)
            for e in range(LO)
        ]
        named = jnp.concatenate(named, axis=0)
        rank_out[g * LO : (g + 1) * LO, :] = named * nn(named.astype(BF), upto)
        pick_rows(rank_out, g, pick_s)
        put_rows(x_out, g, nn(pick_s[...], tok_s[...]), slice(0, LEAD))


def source(first, step):
    return lax.rem(first[0] + step + HI, HI)


def rest_group(first, got, group, begin, count, kept):
    for b in range(PACK):
        at = source(first, STEPS[group * PACK + b]) * SENT_REST + begin
        for f in range(count):
            here = pl.ds(pl.multiple_of(at + f * TOK, 16), TOK)
            kept[b * TOK : (b + 1) * TOK, f * LANES : (f + 1) * LANES] = got[here, :]


def rest_kernel(first, got, rank, ids, out, gate_out, tok_s, cot_s, pick_s):
    base = (first[0] * LO).astype(F32)
    for g in range(GROUPS):
        rest_group(first, got, g, 0, SECOND, tok_s)
        rest_group(first, got, g, AT_COT, CUTS, cot_s)
        part = []
        for b in range(PACK):
            at = source(first, STEPS[g * PACK + b]) * SENT_REST + AT_GATES
            one = got[pl.ds(pl.multiple_of(at, 16), 16), :].astype(F32)
            two = got[pl.ds(pl.multiple_of(at + 16, 16), 16), :].astype(F32)
            part.append((one[:TOP] + one[TOP:]) + two[:TOP])
        gates = jnp.concatenate(part, axis=1)
        named = ids[g * TOP : (g + 1) * TOP, :]
        weight = [
            jnp.sum(jnp.where(named == base + e, gates, 0.0), axis=0, keepdims=True)
            for e in range(LO)
        ]
        gate_out[g * LO : (g + 1) * LO, :] = jnp.concatenate(weight, axis=0)
        pick_rows(rank, g, pick_s)
        scale = []
        for e in range(LO):
            picked = pick_s[e * SLOTS : (e + 1) * SLOTS, :].astype(F32)
            scale.append(jnp.sum(picked * weight[e], axis=1, keepdims=True))
        put_rows(out, g, nn(pick_s[...], tok_s[...]), slice(0, TAIL))
        grads = jnp.concatenate(scale, axis=0) * nn(pick_s[...], cot_s[...])
        put_rows(out, g, grads, slice(TAIL, TAIL + WIDTH))


TILE = 160


def tiles(step):
    def one(i, carry):
        step(pl.ds(pl.multiple_of(i * TILE, 16), TILE))
        return carry

    lax.fori_loop(0, ROWS // TILE, one, 0)


def gated(x, rest, w_gate, w_up, rows):
    tok = jnp.concatenate([x[rows, :], rest[rows, :TAIL]], axis=1)
    gate_pre = nn(tok, w_gate[...])
    up_pre = nn(tok, w_up[...])
    sig = jax.nn.sigmoid(gate_pre)
    activation = gate_pre * sig
    hidden = (activation * up_pre).astype(BF)
    return gate_pre, up_pre, sig, activation, hidden


def forward_kernel(x, rest, w_gate, w_up, w_down, out):
    def step(rows):
        hidden = gated(x, rest, w_gate, w_up, rows)[-1]
        out[rows, :] = nn(hidden, w_down[...]).astype(BF)

    tiles(step)


def backward_kernel(x, rest, w_gate, w_up, w_down, out, weight, hidden_s, gate_s, up_s):
    def step(rows):
        gate_pre, up_pre, sig, activation, hidden = gated(x, rest, w_gate, w_up, rows)
        hidden_grad = nt(rest[rows, TAIL:], w_down[...])
        slope = sig * (1.0 + gate_pre * (1.0 - sig))
        gate = (hidden_grad * up_pre * slope).astype(BF)
        up = (hidden_grad * activation).astype(BF)
        hidden_s[rows, :] = hidden
        gate_s[rows, :] = gate
        up_s[rows, :] = up
        out[rows, :] = (nt(gate, w_gate[...]) + nt(up, w_up[...])).astype(BF)

    tiles(step)
    for n, side in enumerate((gate_s, up_s)):
        at = n * WIDTH
        weight[at : at + LEAD, :] = tn(x[...], side[...]).astype(BF)
        weight[at + LEAD : at + WIDTH, :] = tn(rest[:, :TAIL], side[...]).astype(BF)
    weight[2 * WIDTH : 3 * WIDTH, :] = tn(hidden_s[...], rest[:, TAIL:]).astype(BF)


def split(value):
    high = value.astype(BF)
    return high, (value - high.astype(F32)).astype(BF)


def layer_kernel(first, got, rank, ids, gate, eo, out, picks_out, cot_s, eo_s):
    base = (first[0] * LO).astype(F32)
    expert = lax.broadcasted_iota(jnp.int32, (LO, ALL), 0)
    slot = lax.broadcasted_iota(jnp.int32, (LO, ALL), 1)
    spread = ((slot >= expert * SLOTS) & (slot < (expert + 1) * SLOTS)).astype(F32).astype(BF)
    lane = lax.broadcasted_iota(jnp.int32, (1, ALL), 1)
    place = (lane - SLOTS * lax.div(lane, SLOTS) + 1).astype(F32)
    for g in range(GROUPS):
        rest_group(first, got, g, AT_COT, CUTS, cot_s)
        for e in range(LO):
            at = (e * GROUPS + g) * SLOTS
            eo_s[e * SLOTS : (e + 1) * SLOTS, :] = eo[at : at + SLOTS, :]
        rows = slice(g * LO, (g + 1) * LO)
        picks = tn(rank[rows, :].astype(BF), spread) == place
        picks_out[g * GTOK : (g + 1) * GTOK, :] = jnp.where(picks, 1.0, 0.0).astype(BF)
        high, low = split(gate[rows, :])
        high = jnp.where(picks, tn(high, spread), 0.0).astype(BF)
        low = jnp.where(picks, tn(low, spread), 0.0).astype(BF)
        layer = nn(high, eo_s[...]) + nn(low, eo_s[...])
        along = jnp.where(picks, nt(cot_s[...], eo_s[...]), 0.0)
        high, low = split(along)
        along = nt(spread, high) + nt(spread, low)
        named = ids[g * TOP : (g + 1) * TOP, :]
        grad = jnp.zeros((TOP, GTOK), F32)
        for e in range(LO):
            grad += jnp.where(named == base + e, along[e : e + 1, :], 0.0)
        grad_high = grad.astype(BF).astype(F32)
        grad = jnp.concatenate([grad_high, grad - grad_high], axis=0).astype(BF)
        for b in range(PACK):
            at = source(first, STEPS[g * PACK + b])
            for f in range(CUTS):
                here = layer[b * TOK : (b + 1) * TOK, f * LANES : (f + 1) * LANES]
                out[at, f * TOK : (f + 1) * TOK, :] = here.astype(BF)
            out[at, 2 * WIDTH : BACK, :] = grad[:, b * TOK : (b + 1) * TOK]


def back_kernel(first, picks, ib, held, out, ib_s, sent_s, sems):
    del held
    copies = []
    for g in range(GROUPS):
        for e in range(LO):
            at = (e * GROUPS + g) * SLOTS
            ib_s[e * SLOTS : (e + 1) * SLOTS, :] = ib[at : at + SLOTS, :]
        back = nn(picks[g * GTOK : (g + 1) * GTOK, :], ib_s[...])
        for b in range(PACK):
            n = g * PACK + b
            for f in range(CUTS):
                here = back[b * TOK : (b + 1) * TOK, f * LANES : (f + 1) * LANES]
                sent_s[n, f * TOK : (f + 1) * TOK, :] = here.astype(BF)
            copy = pltpu.make_async_copy(
                sent_s.at[n],
                out.at[source(first, STEPS[n]), pl.ds(WIDTH, WIDTH), :],
                sems.at[n],
            )
            copy.start()
            copies.append(copy)
    for copy in copies:
        copy.wait()


def unpack_kernel(got, layer, back, grad):
    for f in range(CUTS):
        cut = slice(f * LANES, (f + 1) * LANES)
        layer[:, cut] = got[f * TOK : (f + 1) * TOK, :]
        back[:, cut] = got[WIDTH + f * TOK : WIDTH + (f + 1) * TOK, :]
    parts = got[2 * WIDTH : BACK, :].astype(F32)
    grad[...] = parts[:TOP] + parts[TOP:]


def body(tokens, expert_ids, gate_weights, cotangent, w_gate, w_up, w_down):
    shape = jax.ShapeDtypeStruct
    first = lax.axis_index("hi").astype(jnp.int32).reshape(1)
    w_gate, w_up, w_down = w_gate[0], w_up[0], w_down[0]
    square = 2 * ROWS * WIDTH * WIDTH
    ring_sent, rest_sent = call(
        pack_kernel,
        [shape((SENT_RING, LANES), BF), shape((SENT_REST, LANES), BF)],
        [tokens, expert_ids.T, gate_weights.T, cotangent],
        room=56,
    )
    got = lax.all_gather(rest_sent, "hi", axis=0, tiled=True)
    after = [(i, (i + 1) % HI) for i in range(HI)]
    before = [(i, (i - 1) % HI) for i in range(HI)]
    blocks = {0: ring_sent}
    for h in range(1, HI // 2 + 1):
        blocks[-h] = lax.ppermute(blocks[1 - h], "hi", after)
        if h < HI // 2:
            blocks[h] = lax.ppermute(blocks[h - 1], "hi", before)
    picked = pltpu.VMEM((ALL, GTOK), BF)
    rows_first, rank, ids = call(
        first_kernel,
        [
            shape((ROWS, LEAD), BF),
            shape((GROUPS * LO, GTOK), F32),
            shape((GROUPS * TOP, GTOK), F32),
        ],
        [first] + [blocks[s] for s in STEPS],
        [pltpu.VMEM((GTOK, LEAD), BF), picked],
        scalars=1,
    )
    rows_rest, gate = call(
        rest_kernel,
        [shape((ROWS, TAIL + WIDTH), BF), shape((GROUPS * LO, GTOK), F32)],
        [first, got, rank, ids],
        [pltpu.VMEM((GTOK, TAIL), BF), pltpu.VMEM((GTOK, WIDTH), BF), picked],
        scalars=1,
        flops=100 * square,
    )
    exchange = functools.partial(
        lax.all_to_all, axis_name="lo", split_axis=0, concat_axis=0, tiled=True
    )
    x = exchange(rows_first)
    rest = exchange(rows_rest)
    narrow = shape((ROWS, WIDTH), BF)
    (expert_out,) = call(
        forward_kernel, [narrow], [x, rest, w_gate, w_up, w_down], flops=3 * square
    )
    eo = exchange(expert_out)
    whole = pltpu.VMEM((ROWS, WIDTH), BF)
    input_back, weight_part = call(
        backward_kernel,
        [narrow, shape((3 * WIDTH, WIDTH), BF)],
        [x, rest, w_gate, w_up, w_down],
        [whole, whole, whole],
        flops=8 * square,
    )
    eo, input_back = lax.optimization_barrier((eo, input_back))
    ib = exchange(input_back)
    partial, picks = call(
        layer_kernel,
        [shape((HI, BACK, LANES), BF), shape((GROUPS * GTOK, ALL), BF)],
        [first, got, rank, ids, gate, eo],
        [pltpu.VMEM((GTOK, WIDTH), BF), pltpu.VMEM((ALL, WIDTH), BF)],
        scalars=1,
        flops=3 * square,
    )
    partial = pl.pallas_call(
        back_kernel,
        out_shape=shape((HI, BACK, LANES), BF),
        in_specs=[SMEM, VMEM, VMEM, pl.BlockSpec(memory_space=pl.ANY)],
        out_specs=pl.BlockSpec(memory_space=pl.ANY),
        scratch_shapes=[
            pltpu.VMEM((ALL, WIDTH), BF),
            pltpu.VMEM((HI, WIDTH, LANES), BF),
            pltpu.SemaphoreType.DMA((HI,)),
        ],
        input_output_aliases={3: 0},
        compiler_params=pltpu.CompilerParams(vmem_limit_bytes=24 * MIB),
        cost_estimate=pl.CostEstimate(flops=square, bytes_accessed=4 << 20, transcendentals=0),
    )(first, picks, ib, partial)
    summed = lax.psum_scatter(
        partial.reshape(HI * BACK, LANES), "hi", scatter_dimension=0, tiled=True
    )
    over_dp = functools.partial(
        lax.all_to_all, axis_name="dp", split_axis=0, concat_axis=0, tiled=True
    )
    data = lax.axis_size("dp")
    share = over_dp(weight_part).reshape(data, -1, WIDTH).astype(F32)
    grad_scale = float(data * TOK * TOP) ** (-0.5)
    share = (jnp.sum(share, axis=0) * grad_scale).astype(BF)
    weight_grad = over_dp(jnp.tile(share, (data, 1))).reshape(3, 1, WIDTH, WIDTH)
    layer_out, grad_tokens, grad_gates = call(
        unpack_kernel,
        [shape((TOK, WIDTH), BF), shape((TOK, WIDTH), BF), shape((TOP, LANES), F32)],
        [summed],
        room=56,
    )
    return (
        layer_out,
        grad_tokens,
        grad_gates.T,
        weight_grad[0],
        weight_grad[1],
        weight_grad[2],
    )


def solution(mesh):
    data = mesh.shape["dp"]
    cut = Mesh(mesh.devices.reshape(data, HI, LO), ("dp", "hi", "lo"))
    rows = P(("dp", "hi", "lo"), None)
    weight = P(("hi", "lo"), None, None)
    return jax.shard_map(
        body,
        mesh=cut,
        in_specs=(rows, rows, rows, rows, weight, weight, weight),
        out_specs=(rows, rows, rows, weight, weight, weight),
        check_vma=False,
    )
```

```python
import functools
import jax
import jax.numpy as jnp
from jax import lax
from jax.experimental import pallas as pl
from jax.experimental.pallas import tpu as pltpu
from jax.sharding import Mesh, PartitionSpec as P

BF = jnp.bfloat16
F32 = jnp.float32
TOK = 128
WIDTH = 512
TOP = 8
CAP = 20
HI = 8
LO = 8
PACK = 4
GROUPS = HI // PACK
SLOTS = PACK * CAP
GTOK = PACK * TOK
LANES = 128
CUTS = WIDTH // LANES
FIRST = 3
SECOND = CUTS - FIRST
LEAD = FIRST * LANES
TAIL = SECOND * LANES
SENT_LEAD = LEAD + 2 * TOP
SENT_REST = TAIL + WIDTH + 4 * TOP
EARLY = 256
MIXED = TAIL + EARLY
AT_COT = TAIL
AT_GATES = TAIL + WIDTH
BACK = 2 * WIDTH + 2 * TOP
ALL = LO * SLOTS
ROWS = HI * CAP * LO
MIB = 1024 * 1024
VMEM = pl.BlockSpec(memory_space=pltpu.VMEM)
SMEM = pl.BlockSpec(memory_space=pltpu.SMEM)


def nn(a, b):
    return jnp.dot(a, b, preferred_element_type=F32)


def nt(a, b):
    return lax.dot_general(a, b, (((1,), (1,)), ((), ())), preferred_element_type=F32)


def tn(a, b):
    return lax.dot_general(a, b, (((0,), (0,)), ((), ())), preferred_element_type=F32)


def call(kernel, shapes, args, scratch=(), scalars=0, flops=0, room=24):
    moved = sum(a.size * a.dtype.itemsize for a in args)
    moved += sum(s.size * s.dtype.itemsize for s in shapes)
    return pl.pallas_call(
        kernel,
        out_shape=shapes,
        in_specs=[SMEM] * scalars + [VMEM] * (len(args) - scalars),
        out_specs=[VMEM] * len(shapes),
        scratch_shapes=list(scratch),
        compiler_params=pltpu.CompilerParams(vmem_limit_bytes=room * MIB),
        cost_estimate=pl.CostEstimate(flops=flops, bytes_accessed=moved, transcendentals=0),
    )(*args)


def pack_kernel(tok, ids, gates, cot, lead_out, rest_out):
    for f in range(CUTS):
        cut = slice(f * LANES, (f + 1) * LANES)
        to, at = (lead_out, f) if f < FIRST else (rest_out, f - FIRST)
        to[at * TOK : (at + 1) * TOK, :] = tok[:, cut]
        rest_out[AT_COT + f * TOK : AT_COT + (f + 1) * TOK, :] = cot[:, cut]
    gate = gates[...]
    high = gate.astype(BF).astype(F32)
    middle = (gate - high).astype(BF).astype(F32)
    low = gate - high - middle
    named = ids[...].astype(F32)
    lead_out[LEAD : LEAD + 16, :] = jnp.concatenate([named, named], axis=0).astype(BF)
    rest_out[AT_GATES : AT_GATES + 16, :] = jnp.concatenate([high, middle], axis=0).astype(BF)
    rest_out[AT_GATES + 16 : AT_GATES + 32, :] = jnp.concatenate([low, low], axis=0).astype(BF)


def upper(size):
    row = lax.broadcasted_iota(jnp.int32, (size, size), 0)
    col = lax.broadcasted_iota(jnp.int32, (size, size), 1)
    return (row <= col).astype(F32).astype(BF)


def place_rows():
    return (lax.broadcasted_iota(jnp.int32, (SLOTS, GTOK), 0) + 1).astype(F32)


def pick_rows(rank, group, pick_s):
    place = place_rows()
    for e in range(LO):
        picks = rank[group * LO + e : group * LO + e + 1, :] == place
        pick_s[e * SLOTS : (e + 1) * SLOTS, :] = jnp.where(picks, 1.0, 0.0).astype(BF)


def put_rows(out, group, rows, lanes):
    for e in range(LO):
        to = (e * GROUPS + group) * SLOTS
        out[to : to + SLOTS, lanes] = rows[e * SLOTS : (e + 1) * SLOTS, :].astype(BF)


def first_kernel(first, got, x_out, rank_out, ids_out, tok_s, pick_s):
    base = (first[0] * LO).astype(F32)
    upto = upper(GTOK)
    for g in range(GROUPS):
        part = []
        for b in range(PACK):
            at = (g * PACK + b) * SENT_LEAD
            for f in range(FIRST):
                cut = slice(f * LANES, (f + 1) * LANES)
                tok_s[b * TOK : (b + 1) * TOK, cut] = got[at + f * TOK : at + (f + 1) * TOK, :]
            part.append(got[at + LEAD : at + LEAD + 16, :].astype(F32)[:TOP])
        ids = jnp.concatenate(part, axis=1)
        ids_out[g * TOP : (g + 1) * TOP, :] = ids
        named = [
            jnp.sum(jnp.where(ids == base + e, 1.0, 0.0), axis=0, keepdims=True)
            for e in range(LO)
        ]
        named = jnp.concatenate(named, axis=0)
        rank_out[g * LO : (g + 1) * LO, :] = named * nn(named.astype(BF), upto)
        pick_rows(rank_out, g, pick_s)
        put_rows(x_out, g, nn(pick_s[...], tok_s[...]), slice(0, LEAD))


def rest_group(got, group, begin, count, kept):
    for b in range(PACK):
        at = (group * PACK + b) * SENT_REST + begin
        for f in range(count):
            cut = slice(f * LANES, (f + 1) * LANES)
            kept[b * TOK : (b + 1) * TOK, cut] = got[at + f * TOK : at + (f + 1) * TOK, :]


def rest_kernel(first, got, rank, ids, out, late_out, gate_out, tok_s, cot_s, pick_s):
    base = (first[0] * LO).astype(F32)
    for g in range(GROUPS):
        rest_group(got, g, 0, SECOND, tok_s)
        rest_group(got, g, AT_COT, CUTS, cot_s)
        part = []
        for b in range(PACK):
            at = (g * PACK + b) * SENT_REST + AT_GATES
            one = got[at : at + 16, :].astype(F32)
            two = got[at + 16 : at + 32, :].astype(F32)
            part.append((one[:TOP] + one[TOP:]) + two[:TOP])
        gates = jnp.concatenate(part, axis=1)
        named = ids[g * TOP : (g + 1) * TOP, :]
        weight = [
            jnp.sum(jnp.where(named == base + e, gates, 0.0), axis=0, keepdims=True)
            for e in range(LO)
        ]
        gate_out[g * LO : (g + 1) * LO, :] = jnp.concatenate(weight, axis=0)
        pick_rows(rank, g, pick_s)
        scale = []
        for e in range(LO):
            picked = pick_s[e * SLOTS : (e + 1) * SLOTS, :].astype(F32)
            scale.append(jnp.sum(picked * weight[e], axis=1, keepdims=True))
        put_rows(out, g, nn(pick_s[...], tok_s[...]), slice(0, TAIL))
        grads = jnp.concatenate(scale, axis=0) * nn(pick_s[...], cot_s[...])
        put_rows(out, g, grads[:, :EARLY], slice(TAIL, MIXED))
        put_rows(late_out, g, grads[:, EARLY:], slice(0, WIDTH - EARLY))


TILE = 160


def tiles(step):
    def one(i, carry):
        step(pl.ds(pl.multiple_of(i * TILE, 16), TILE))
        return carry

    lax.fori_loop(0, ROWS // TILE, one, 0)


def gated(x, rest, w_gate, w_up, rows):
    tok = jnp.concatenate([x[rows, :], rest[rows, :TAIL]], axis=1)
    gate_pre = nn(tok, w_gate[...])
    up_pre = nn(tok, w_up[...])
    sig = jax.nn.sigmoid(gate_pre)
    activation = gate_pre * sig
    hidden = (activation * up_pre).astype(BF)
    return gate_pre, up_pre, sig, activation, hidden


def forward_kernel(x, rest, w_gate, w_up, w_down, out):
    def step(rows):
        hidden = gated(x, rest, w_gate, w_up, rows)[-1]
        out[rows, :] = nn(hidden, w_down[...]).astype(BF)

    tiles(step)


def backward_kernel(x, rest, late, w_gate, w_up, w_down, out, weight, hidden_s, gate_s, up_s):
    def step(rows):
        gate_pre, up_pre, sig, activation, hidden = gated(x, rest, w_gate, w_up, rows)
        grads = jnp.concatenate([rest[rows, TAIL:], late[rows, :]], axis=1)
        hidden_grad = nt(grads, w_down[...])
        slope = sig * (1.0 + gate_pre * (1.0 - sig))
        gate = (hidden_grad * up_pre * slope).astype(BF)
        up = (hidden_grad * activation).astype(BF)
        hidden_s[rows, :] = hidden
        gate_s[rows, :] = gate
        up_s[rows, :] = up
        out[rows, :] = (nt(gate, w_gate[...]) + nt(up, w_up[...])).astype(BF)

    tiles(step)
    for n, side in enumerate((gate_s, up_s)):
        at = n * WIDTH
        weight[at : at + LEAD, :] = tn(x[...], side[...]).astype(BF)
        weight[at + LEAD : at + WIDTH, :] = tn(rest[:, :TAIL], side[...]).astype(BF)
    weight[2 * WIDTH :, :EARLY] = tn(hidden_s[...], rest[:, TAIL:]).astype(BF)
    weight[2 * WIDTH :, EARLY:] = tn(hidden_s[...], late[...]).astype(BF)


def split(value):
    high = value.astype(BF)
    return high, (value - high.astype(F32)).astype(BF)


def layer_kernel(first, got, rank, ids, gate, eo, out, picks_out, cot_s, eo_s):
    base = (first[0] * LO).astype(F32)
    expert = lax.broadcasted_iota(jnp.int32, (LO, ALL), 0)
    slot = lax.broadcasted_iota(jnp.int32, (LO, ALL), 1)
    spread = ((slot >= expert * SLOTS) & (slot < (expert + 1) * SLOTS)).astype(F32).astype(BF)
    lane = lax.broadcasted_iota(jnp.int32, (1, ALL), 1)
    place = (lane - SLOTS * lax.div(lane, SLOTS) + 1).astype(F32)
    for g in range(GROUPS):
        rest_group(got, g, AT_COT, CUTS, cot_s)
        for e in range(LO):
            at = (e * GROUPS + g) * SLOTS
            eo_s[e * SLOTS : (e + 1) * SLOTS, :] = eo[at : at + SLOTS, :]
        rows = slice(g * LO, (g + 1) * LO)
        picks = tn(rank[rows, :].astype(BF), spread) == place
        picks_out[g * GTOK : (g + 1) * GTOK, :] = jnp.where(picks, 1.0, 0.0).astype(BF)
        high, low = split(gate[rows, :])
        high = jnp.where(picks, tn(high, spread), 0.0).astype(BF)
        low = jnp.where(picks, tn(low, spread), 0.0).astype(BF)
        layer = nn(high, eo_s[...]) + nn(low, eo_s[...])
        along = jnp.where(picks, nt(cot_s[...], eo_s[...]), 0.0)
        high, low = split(along)
        along = nt(spread, high) + nt(spread, low)
        named = ids[g * TOP : (g + 1) * TOP, :]
        grad = jnp.zeros((TOP, GTOK), F32)
        for e in range(LO):
            grad += jnp.where(named == base + e, along[e : e + 1, :], 0.0)
        grad_high = grad.astype(BF).astype(F32)
        grad = jnp.concatenate([grad_high, grad - grad_high], axis=0).astype(BF)
        for b in range(PACK):
            at = g * PACK + b
            for f in range(CUTS):
                here = layer[b * TOK : (b + 1) * TOK, f * LANES : (f + 1) * LANES]
                out[at, f * TOK : (f + 1) * TOK, :] = here.astype(BF)
            out[at, 2 * WIDTH : BACK, :] = grad[:, b * TOK : (b + 1) * TOK]


def back_kernel(picks, ib, held, out, ib_s, sent_s, sems):
    del held
    copies = []
    for g in range(GROUPS):
        for e in range(LO):
            at = (e * GROUPS + g) * SLOTS
            ib_s[e * SLOTS : (e + 1) * SLOTS, :] = ib[at : at + SLOTS, :]
        back = nn(picks[g * GTOK : (g + 1) * GTOK, :], ib_s[...])
        for b in range(PACK):
            n = g * PACK + b
            for f in range(CUTS):
                here = back[b * TOK : (b + 1) * TOK, f * LANES : (f + 1) * LANES]
                sent_s[n, f * TOK : (f + 1) * TOK, :] = here.astype(BF)
            copy = pltpu.make_async_copy(
                sent_s.at[n],
                out.at[n, pl.ds(WIDTH, WIDTH), :],
                sems.at[n],
            )
            copy.start()
            copies.append(copy)
    for copy in copies:
        copy.wait()


def unpack_kernel(got, layer, back, grad):
    for f in range(CUTS):
        cut = slice(f * LANES, (f + 1) * LANES)
        layer[:, cut] = got[f * TOK : (f + 1) * TOK, :]
        back[:, cut] = got[WIDTH + f * TOK : WIDTH + (f + 1) * TOK, :]
    parts = got[2 * WIDTH : BACK, :].astype(F32)
    grad[...] = parts[:TOP] + parts[TOP:]


def body(tokens, expert_ids, gate_weights, cotangent, w_gate, w_up, w_down):
    shape = jax.ShapeDtypeStruct
    first = lax.axis_index("hi").astype(jnp.int32).reshape(1)
    w_gate, w_up, w_down = w_gate[0], w_up[0], w_down[0]
    square = 2 * ROWS * WIDTH * WIDTH
    lead_sent, rest_sent = call(
        pack_kernel,
        [shape((SENT_LEAD, LANES), BF), shape((SENT_REST, LANES), BF)],
        [tokens, expert_ids.T, gate_weights.T, cotangent],
        room=56,
    )
    got = lax.all_gather(rest_sent, "hi", axis=0, tiled=True)
    lead = lax.all_gather(lead_sent, "hi", axis=0, tiled=True)
    picked = pltpu.VMEM((ALL, GTOK), BF)
    rows_first, rank, ids = call(
        first_kernel,
        [
            shape((ROWS, LEAD), BF),
            shape((GROUPS * LO, GTOK), F32),
            shape((GROUPS * TOP, GTOK), F32),
        ],
        [first, lead],
        [pltpu.VMEM((GTOK, LEAD), BF), picked],
        scalars=1,
    )
    rows_rest, rows_late, gate = call(
        rest_kernel,
        [
            shape((ROWS, MIXED), BF),
            shape((ROWS, WIDTH - EARLY), BF),
            shape((GROUPS * LO, GTOK), F32),
        ],
        [first, got, rank, ids],
        [pltpu.VMEM((GTOK, TAIL), BF), pltpu.VMEM((GTOK, WIDTH), BF), picked],
        scalars=1,
        flops=100 * square,
    )
    exchange = functools.partial(
        lax.all_to_all, axis_name="lo", split_axis=0, concat_axis=0, tiled=True
    )
    x = exchange(rows_first)
    rest = exchange(rows_rest)
    late = exchange(rows_late)
    narrow = shape((ROWS, WIDTH), BF)
    (expert_out,) = call(
        forward_kernel, [narrow], [x, rest, w_gate, w_up, w_down], flops=3 * square
    )
    eo = exchange(expert_out)
    whole = pltpu.VMEM((ROWS, WIDTH), BF)
    input_back, weight_part = call(
        backward_kernel,
        [narrow, shape((3 * WIDTH, WIDTH), BF)],
        [x, rest, late, w_gate, w_up, w_down],
        [whole, whole, whole],
        flops=8 * square,
    )
    eo, input_back = lax.optimization_barrier((eo, input_back))
    ib = exchange(input_back)
    partial, picks = call(
        layer_kernel,
        [shape((HI, BACK, LANES), BF), shape((GROUPS * GTOK, ALL), BF)],
        [first, got, rank, ids, gate, eo],
        [pltpu.VMEM((GTOK, WIDTH), BF), pltpu.VMEM((ALL, WIDTH), BF)],
        scalars=1,
        flops=3 * square,
    )
    partial = pl.pallas_call(
        back_kernel,
        out_shape=shape((HI, BACK, LANES), BF),
        in_specs=[VMEM, VMEM, pl.BlockSpec(memory_space=pl.ANY)],
        out_specs=pl.BlockSpec(memory_space=pl.ANY),
        scratch_shapes=[
            pltpu.VMEM((ALL, WIDTH), BF),
            pltpu.VMEM((HI, WIDTH, LANES), BF),
            pltpu.SemaphoreType.DMA((HI,)),
        ],
        input_output_aliases={2: 0},
        compiler_params=pltpu.CompilerParams(vmem_limit_bytes=24 * MIB),
        cost_estimate=pl.CostEstimate(flops=square, bytes_accessed=4 << 20, transcendentals=0),
    )(picks, ib, partial)
    summed = lax.psum_scatter(
        partial.reshape(HI * BACK, LANES), "hi", scatter_dimension=0, tiled=True
    )
    over_dp = functools.partial(
        lax.all_to_all, axis_name="dp", split_axis=0, concat_axis=0, tiled=True
    )
    data = lax.axis_size("dp")
    share = over_dp(weight_part).reshape(data, -1, WIDTH).astype(F32)
    grad_scale = float(data * TOK * TOP) ** (-0.5)
    share = (jnp.sum(share, axis=0) * grad_scale).astype(BF)
    weight_grad = over_dp(jnp.tile(share, (data, 1))).reshape(3, 1, WIDTH, WIDTH)
    layer_out, grad_tokens, grad_gates = call(
        unpack_kernel,
        [shape((TOK, WIDTH), BF), shape((TOK, WIDTH), BF), shape((TOP, LANES), F32)],
        [summed],
        room=56,
    )
    return (
        layer_out,
        grad_tokens,
        grad_gates.T,
        weight_grad[0],
        weight_grad[1],
        weight_grad[2],
    )


def solution(mesh):
    data = mesh.shape["dp"]
    cut = Mesh(mesh.devices.reshape(data, HI, LO), ("dp", "hi", "lo"))
    rows = P(("dp", "hi", "lo"), None)
    weight = P(("hi", "lo"), None, None)
    return jax.shard_map(
        body,
        mesh=cut,
        in_specs=(rows, rows, rows, rows, weight, weight, weight),
        out_specs=(rows, rows, rows, weight, weight, weight),
        check_vma=False,
    )
```

```python
import functools
import jax
import jax.numpy as jnp
from jax import lax
from jax.experimental import pallas as pl
from jax.experimental.pallas import tpu as pltpu
from jax.sharding import Mesh, PartitionSpec as P

BF = jnp.bfloat16
F32 = jnp.float32
TOK = 128
WIDTH = 512
TOP = 8
CAP = 20
HI = 8
LO = 8
PACK = 4
GROUPS = HI // PACK
SLOTS = PACK * CAP
GTOK = PACK * TOK
LANES = 128
CUTS = WIDTH // LANES
FIRST = 3
SECOND = CUTS - FIRST
LEAD = FIRST * LANES
TAIL = SECOND * LANES
PART = TOK // 2
AT_IDS = LEAD + PART
SENT_LEAD = AT_IDS + 4 * TOP
SENT_REST = TOK - PART + WIDTH
EARLY = 256
MIXED = TAIL + EARLY
AT_COT = TOK - PART
BACK = 2 * WIDTH + 2 * TOP
ALL = LO * SLOTS
ROWS = HI * CAP * LO
MIB = 1024 * 1024
ROOM = 24
VMEM = pl.BlockSpec(memory_space=pltpu.VMEM)
SMEM = pl.BlockSpec(memory_space=pltpu.SMEM)


def nn(a, b):
    return jnp.dot(a, b, preferred_element_type=F32)


def nt(a, b):
    return lax.dot_general(a, b, (((1,), (1,)), ((), ())), preferred_element_type=F32)


def tn(a, b):
    return lax.dot_general(a, b, (((0,), (0,)), ((), ())), preferred_element_type=F32)


def call(kernel, shapes, args, scratch=(), scalars=0, flops=0, room=24):
    moved = sum(a.size * a.dtype.itemsize for a in args)
    moved += sum(s.size * s.dtype.itemsize for s in shapes)
    return pl.pallas_call(
        kernel,
        out_shape=shapes,
        in_specs=[SMEM] * scalars + [VMEM] * (len(args) - scalars),
        out_specs=[VMEM] * len(shapes),
        scratch_shapes=list(scratch),
        compiler_params=pltpu.CompilerParams(vmem_limit_bytes=room * MIB),
        cost_estimate=pl.CostEstimate(flops=flops, bytes_accessed=moved, transcendentals=0),
    )(*args)


def pack_kernel(tok, ids, gates, cot, lead_out, rest_out):
    for f in range(CUTS):
        cut = slice(f * LANES, (f + 1) * LANES)
        if f < FIRST:
            lead_out[f * TOK : (f + 1) * TOK, :] = tok[:, cut]
        rest_out[AT_COT + f * TOK : AT_COT + (f + 1) * TOK, :] = cot[:, cut]
    lead_out[LEAD:AT_IDS, :] = tok[:PART, LEAD:]
    rest_out[:AT_COT, :] = tok[PART:, LEAD:]
    gate = gates[...]
    high = gate.astype(BF).astype(F32)
    middle = (gate - high).astype(BF).astype(F32)
    low = gate - high - middle
    named = ids[...].astype(F32)
    lead_out[AT_IDS : AT_IDS + 16, :] = jnp.concatenate([named, high], axis=0).astype(BF)
    lead_out[AT_IDS + 16 : SENT_LEAD, :] = jnp.concatenate([middle, low], axis=0).astype(BF)


def upper(size):
    row = lax.broadcasted_iota(jnp.int32, (size, size), 0)
    col = lax.broadcasted_iota(jnp.int32, (size, size), 1)
    return (row <= col).astype(F32).astype(BF)


def place_rows():
    return (lax.broadcasted_iota(jnp.int32, (SLOTS, GTOK), 0) + 1).astype(F32)


def pick_rows(rank, group, pick_s):
    place = place_rows()
    for e in range(LO):
        picks = rank[group * LO + e : group * LO + e + 1, :] == place
        pick_s[e * SLOTS : (e + 1) * SLOTS, :] = jnp.where(picks, 1.0, 0.0).astype(BF)


def put_rows(out, group, rows, lanes):
    for e in range(LO):
        to = (e * GROUPS + group) * SLOTS
        out[to : to + SLOTS, lanes] = rows[e * SLOTS : (e + 1) * SLOTS, :].astype(BF)


def first_kernel(first, got, x_out, rank_out, ids_out, gate_out, tok_s, pick_s):
    base = (first[0] * LO).astype(F32)
    upto = upper(GTOK)
    for g in range(GROUPS):
        named, weights = [], []
        for b in range(PACK):
            at = (g * PACK + b) * SENT_LEAD
            for f in range(FIRST):
                cut = slice(f * LANES, (f + 1) * LANES)
                tok_s[b * TOK : (b + 1) * TOK, cut] = got[at + f * TOK : at + (f + 1) * TOK, :]
            one = got[at + AT_IDS : at + AT_IDS + 16, :].astype(F32)
            two = got[at + AT_IDS + 16 : at + SENT_LEAD, :].astype(F32)
            named.append(one[:TOP])
            weights.append((one[TOP:] + two[:TOP]) + two[TOP:])
        ids = jnp.concatenate(named, axis=1)
        weights = jnp.concatenate(weights, axis=1)
        ids_out[g * TOP : (g + 1) * TOP, :] = ids
        named, weight = [], []
        for e in range(LO):
            same = ids == base + e
            named.append(jnp.sum(jnp.where(same, 1.0, 0.0), axis=0, keepdims=True))
            weight.append(jnp.sum(jnp.where(same, weights, 0.0), axis=0, keepdims=True))
        named = jnp.concatenate(named, axis=0)
        gate_out[g * LO : (g + 1) * LO, :] = jnp.concatenate(weight, axis=0)
        rank_out[g * LO : (g + 1) * LO, :] = named * nn(named.astype(BF), upto)
        pick_rows(rank_out, g, pick_s)
        put_rows(x_out, g, nn(pick_s[...], tok_s[...]), slice(0, LEAD))


def cotangents(got, group, kept):
    for b in range(PACK):
        at = (group * PACK + b) * SENT_REST + AT_COT
        for f in range(CUTS):
            cut = slice(f * LANES, (f + 1) * LANES)
            kept[b * TOK : (b + 1) * TOK, cut] = got[at + f * TOK : at + (f + 1) * TOK, :]


def rest_kernel(lead, got, rank, gate, out, late_out, tok_s, cot_s, pick_s):
    for g in range(GROUPS):
        cotangents(got, g, cot_s)
        for b in range(PACK):
            at = (g * PACK + b) * SENT_LEAD
            tok_s[b * TOK : b * TOK + PART, :] = lead[at + LEAD : at + AT_IDS, :]
            at = (g * PACK + b) * SENT_REST
            tok_s[b * TOK + PART : (b + 1) * TOK, :] = got[at : at + AT_COT, :]
        pick_rows(rank, g, pick_s)
        scale = []
        for e in range(LO):
            picked = pick_s[e * SLOTS : (e + 1) * SLOTS, :].astype(F32)
            weight = gate[g * LO + e : g * LO + e + 1, :]
            scale.append(jnp.sum(picked * weight, axis=1, keepdims=True))
        put_rows(out, g, nn(pick_s[...], tok_s[...]), slice(0, TAIL))
        grads = jnp.concatenate(scale, axis=0) * nn(pick_s[...], cot_s[...])
        put_rows(out, g, grads[:, :EARLY], slice(TAIL, MIXED))
        put_rows(late_out, g, grads[:, EARLY:], slice(0, WIDTH - EARLY))


TILE = 160


def tiles(step):
    def one(i, carry):
        step(pl.ds(pl.multiple_of(i * TILE, 16), TILE))
        return carry

    lax.fori_loop(0, ROWS // TILE, one, 0)


def gated(x, rest, w_gate, w_up, rows):
    tok = jnp.concatenate([x[rows, :], rest[rows, :TAIL]], axis=1)
    gate_pre = nn(tok, w_gate[...])
    up_pre = nn(tok, w_up[...])
    sig = jax.nn.sigmoid(gate_pre)
    activation = gate_pre * sig
    hidden = (activation * up_pre).astype(BF)
    return gate_pre, up_pre, sig, activation, hidden


def forward_kernel(x, rest, w_gate, w_up, w_down, out):
    def step(rows):
        hidden = gated(x, rest, w_gate, w_up, rows)[-1]
        out[rows, :] = nn(hidden, w_down[...]).astype(BF)

    tiles(step)


def backward_kernel(x, rest, late, w_gate, w_up, w_down, out, weight, hidden_s, gate_s, up_s):
    def step(rows):
        gate_pre, up_pre, sig, activation, hidden = gated(x, rest, w_gate, w_up, rows)
        grads = jnp.concatenate([rest[rows, TAIL:], late[rows, :]], axis=1)
        hidden_grad = nt(grads, w_down[...])
        slope = sig * (1.0 + gate_pre * (1.0 - sig))
        gate = (hidden_grad * up_pre * slope).astype(BF)
        up = (hidden_grad * activation).astype(BF)
        hidden_s[rows, :] = hidden
        gate_s[rows, :] = gate
        up_s[rows, :] = up
        out[rows, :] = (nt(gate, w_gate[...]) + nt(up, w_up[...])).astype(BF)

    tiles(step)
    for n, side in enumerate((gate_s, up_s)):
        at = n * WIDTH
        weight[at : at + LEAD, :] = tn(x[...], side[...]).astype(BF)
        weight[at + LEAD : at + WIDTH, :] = tn(rest[:, :TAIL], side[...]).astype(BF)
    weight[2 * WIDTH :, :EARLY] = tn(hidden_s[...], rest[:, TAIL:]).astype(BF)
    weight[2 * WIDTH :, EARLY:] = tn(hidden_s[...], late[...]).astype(BF)


def split(value):
    high = value.astype(BF)
    return high, (value - high.astype(F32)).astype(BF)


def layer_kernel(first, got, rank, ids, gate, eo, out, picks_out, cot_s, eo_s):
    base = (first[0] * LO).astype(F32)
    expert = lax.broadcasted_iota(jnp.int32, (LO, ALL), 0)
    slot = lax.broadcasted_iota(jnp.int32, (LO, ALL), 1)
    spread = ((slot >= expert * SLOTS) & (slot < (expert + 1) * SLOTS)).astype(F32).astype(BF)
    lane = lax.broadcasted_iota(jnp.int32, (1, ALL), 1)
    place = (lane - SLOTS * lax.div(lane, SLOTS) + 1).astype(F32)
    for g in range(GROUPS):
        cotangents(got, g, cot_s)
        for e in range(LO):
            at = (e * GROUPS + g) * SLOTS
            eo_s[e * SLOTS : (e + 1) * SLOTS, :] = eo[at : at + SLOTS, :]
        rows = slice(g * LO, (g + 1) * LO)
        picks = tn(rank[rows, :].astype(BF), spread) == place
        picks_out[g * GTOK : (g + 1) * GTOK, :] = jnp.where(picks, 1.0, 0.0).astype(BF)
        high, low = split(gate[rows, :])
        high = jnp.where(picks, tn(high, spread), 0.0).astype(BF)
        low = jnp.where(picks, tn(low, spread), 0.0).astype(BF)
        layer = nn(high, eo_s[...]) + nn(low, eo_s[...])
        along = jnp.where(picks, nt(cot_s[...], eo_s[...]), 0.0)
        high, low = split(along)
        along = nt(spread, high) + nt(spread, low)
        named = ids[g * TOP : (g + 1) * TOP, :]
        grad = jnp.zeros((TOP, GTOK), F32)
        for e in range(LO):
            grad += jnp.where(named == base + e, along[e : e + 1, :], 0.0)
        grad_high = grad.astype(BF).astype(F32)
        grad = jnp.concatenate([grad_high, grad - grad_high], axis=0).astype(BF)
        for b in range(PACK):
            at = g * PACK + b
            for f in range(CUTS):
                here = layer[b * TOK : (b + 1) * TOK, f * LANES : (f + 1) * LANES]
                out[at, f * TOK : (f + 1) * TOK, :] = here.astype(BF)
            out[at, 2 * WIDTH : BACK, :] = grad[:, b * TOK : (b + 1) * TOK]


def back_kernel(picks, ib, held, out, ib_s, sent_s, sems):
    del held
    copies = []
    for g in range(GROUPS):
        for e in range(LO):
            at = (e * GROUPS + g) * SLOTS
            ib_s[e * SLOTS : (e + 1) * SLOTS, :] = ib[at : at + SLOTS, :]
        back = nn(picks[g * GTOK : (g + 1) * GTOK, :], ib_s[...])
        for b in range(PACK):
            n = g * PACK + b
            for f in range(CUTS):
                here = back[b * TOK : (b + 1) * TOK, f * LANES : (f + 1) * LANES]
                sent_s[n, f * TOK : (f + 1) * TOK, :] = here.astype(BF)
            copy = pltpu.make_async_copy(
                sent_s.at[n],
                out.at[n, pl.ds(WIDTH, WIDTH), :],
                sems.at[n],
            )
            copy.start()
            copies.append(copy)
    for copy in copies:
        copy.wait()


def unpack_kernel(got, layer, back, grad):
    for f in range(CUTS):
        cut = slice(f * LANES, (f + 1) * LANES)
        layer[:, cut] = got[f * TOK : (f + 1) * TOK, :]
        back[:, cut] = got[WIDTH + f * TOK : WIDTH + (f + 1) * TOK, :]
    parts = got[2 * WIDTH : BACK, :].astype(F32)
    grad[...] = parts[:TOP] + parts[TOP:]


def body(tokens, expert_ids, gate_weights, cotangent, w_gate, w_up, w_down):
    shape = jax.ShapeDtypeStruct
    first = lax.axis_index("hi").astype(jnp.int32).reshape(1)
    w_gate, w_up, w_down = w_gate[0], w_up[0], w_down[0]
    square = 2 * ROWS * WIDTH * WIDTH
    lead_sent, rest_sent = call(
        pack_kernel,
        [shape((SENT_LEAD, LANES), BF), shape((SENT_REST, LANES), BF)],
        [tokens, expert_ids.T, gate_weights.T, cotangent],
        room=56,
    )
    got = lax.all_gather(rest_sent, "hi", axis=0, tiled=True)
    lead = lax.all_gather(lead_sent, "hi", axis=0, tiled=True)
    picked = pltpu.VMEM((ALL, GTOK), BF)
    small = shape((GROUPS * LO, GTOK), F32)
    rows_first, rank, ids, gate = call(
        first_kernel,
        [shape((ROWS, LEAD), BF), small, shape((GROUPS * TOP, GTOK), F32), small],
        [first, lead],
        [pltpu.VMEM((GTOK, LEAD), BF), picked],
        scalars=1,
    )
    rows_rest, rows_late = call(
        rest_kernel,
        [shape((ROWS, MIXED), BF), shape((ROWS, WIDTH - EARLY), BF)],
        [lead, got, rank, gate],
        [pltpu.VMEM((GTOK, TAIL), BF), pltpu.VMEM((GTOK, WIDTH), BF), picked],
        flops=100 * square,
        room=ROOM,
    )
    exchange = functools.partial(
        lax.all_to_all, axis_name="lo", split_axis=0, concat_axis=0, tiled=True
    )
    x = exchange(rows_first)
    rest = exchange(rows_rest)
    late = exchange(rows_late)
    narrow = shape((ROWS, WIDTH), BF)
    (expert_out,) = call(
        forward_kernel, [narrow], [x, rest, w_gate, w_up, w_down], flops=3 * square
    )
    eo = exchange(expert_out)
    whole = pltpu.VMEM((ROWS, WIDTH), BF)
    input_back, weight_part = call(
        backward_kernel,
        [narrow, shape((3 * WIDTH, WIDTH), BF)],
        [x, rest, late, w_gate, w_up, w_down],
        [whole, whole, whole],
        flops=8 * square,
        room=ROOM,
    )
    eo, input_back = lax.optimization_barrier((eo, input_back))
    ib = exchange(input_back)
    partial, picks = call(
        layer_kernel,
        [shape((HI, BACK, LANES), BF), shape((GROUPS * GTOK, ALL), BF)],
        [first, got, rank, ids, gate, eo],
        [pltpu.VMEM((GTOK, WIDTH), BF), pltpu.VMEM((ALL, WIDTH), BF)],
        scalars=1,
        room=ROOM,
        flops=3 * square,
    )
    partial = pl.pallas_call(
        back_kernel,
        out_shape=shape((HI, BACK, LANES), BF),
        in_specs=[VMEM, VMEM, pl.BlockSpec(memory_space=pl.ANY)],
        out_specs=pl.BlockSpec(memory_space=pl.ANY),
        scratch_shapes=[
            pltpu.VMEM((ALL, WIDTH), BF),
            pltpu.VMEM((HI, WIDTH, LANES), BF),
            pltpu.SemaphoreType.DMA((HI,)),
        ],
        input_output_aliases={2: 0},
        compiler_params=pltpu.CompilerParams(vmem_limit_bytes=24 * MIB),
        cost_estimate=pl.CostEstimate(flops=square, bytes_accessed=4 << 20, transcendentals=0),
    )(picks, ib, partial)
    summed = lax.psum_scatter(
        partial.reshape(HI * BACK, LANES), "hi", scatter_dimension=0, tiled=True
    )
    over_dp = functools.partial(
        lax.all_to_all, axis_name="dp", split_axis=0, concat_axis=0, tiled=True
    )
    data = lax.axis_size("dp")
    share = over_dp(weight_part).reshape(data, -1, WIDTH).astype(F32)
    grad_scale = float(data * TOK * TOP) ** (-0.5)
    share = (jnp.sum(share, axis=0) * grad_scale).astype(BF)
    weight_grad = over_dp(jnp.tile(share, (data, 1))).reshape(3, 1, WIDTH, WIDTH)
    layer_out, grad_tokens, grad_gates = call(
        unpack_kernel,
        [shape((TOK, WIDTH), BF), shape((TOK, WIDTH), BF), shape((TOP, LANES), F32)],
        [summed],
        room=56,
    )
    return (
        layer_out,
        grad_tokens,
        grad_gates.T,
        weight_grad[0],
        weight_grad[1],
        weight_grad[2],
    )


def solution(mesh):
    data = mesh.shape["dp"]
    cut = Mesh(mesh.devices.reshape(data, HI, LO), ("dp", "hi", "lo"))
    rows = P(("dp", "hi", "lo"), None)
    weight = P(("hi", "lo"), None, None)
    return jax.shard_map(
        body,
        mesh=cut,
        in_specs=(rows, rows, rows, rows, weight, weight, weight),
        out_specs=(rows, rows, rows, weight, weight, weight),
        check_vma=False,
    )
```

```python
import functools
import jax
import jax.numpy as jnp
from jax import lax
from jax.experimental import pallas as pl
from jax.experimental.pallas import tpu as pltpu
from jax.sharding import Mesh, PartitionSpec as P

BF = jnp.bfloat16
F32 = jnp.float32
TOK = 128
WIDTH = 512
TOP = 8
CAP = 20
HI = 8
LO = 8
PACK = 4
GROUPS = HI // PACK
SLOTS = PACK * CAP
GTOK = PACK * TOK
LANES = 128
CUTS = WIDTH // LANES
FIRST = 3
SECOND = CUTS - FIRST
LEAD = FIRST * LANES
TAIL = SECOND * LANES
PART = TOK // 2
AT_IDS = LEAD + PART
SENT_LEAD = AT_IDS + 4 * TOP
SENT_REST = TOK - PART + WIDTH
EARLY = 256
MIXED = TAIL + EARLY
AT_COT = TOK - PART
BACK = 2 * WIDTH + 2 * TOP
ALL = LO * SLOTS
ROWS = HI * CAP * LO
MIB = 1024 * 1024
ROOM = 24
VMEM = pl.BlockSpec(memory_space=pltpu.VMEM)
SMEM = pl.BlockSpec(memory_space=pltpu.SMEM)


def nn(a, b):
    return jnp.dot(a, b, preferred_element_type=F32)


def nt(a, b):
    return lax.dot_general(a, b, (((1,), (1,)), ((), ())), preferred_element_type=F32)


def tn(a, b):
    return lax.dot_general(a, b, (((0,), (0,)), ((), ())), preferred_element_type=F32)


def call(kernel, shapes, args, scratch=(), scalars=0, flops=0, room=24):
    moved = sum(a.size * a.dtype.itemsize for a in args)
    moved += sum(s.size * s.dtype.itemsize for s in shapes)
    return pl.pallas_call(
        kernel,
        out_shape=shapes,
        in_specs=[SMEM] * scalars + [VMEM] * (len(args) - scalars),
        out_specs=[VMEM] * len(shapes),
        scratch_shapes=list(scratch),
        compiler_params=pltpu.CompilerParams(vmem_limit_bytes=room * MIB),
        cost_estimate=pl.CostEstimate(flops=flops, bytes_accessed=moved, transcendentals=0),
    )(*args)


def pack_kernel(tok, ids, gates, cot, lead_out, rest_out):
    for f in range(CUTS):
        cut = slice(f * LANES, (f + 1) * LANES)
        if f < FIRST:
            lead_out[f * TOK : (f + 1) * TOK, :] = tok[:, cut]
        rest_out[AT_COT + f * TOK : AT_COT + (f + 1) * TOK, :] = cot[:, cut]
    lead_out[LEAD:AT_IDS, :] = tok[:PART, LEAD:]
    rest_out[:AT_COT, :] = tok[PART:, LEAD:]
    gate = gates[...]
    high = gate.astype(BF).astype(F32)
    middle = (gate - high).astype(BF).astype(F32)
    low = gate - high - middle
    named = ids[...].astype(F32)
    lead_out[AT_IDS : AT_IDS + 16, :] = jnp.concatenate([named, high], axis=0).astype(BF)
    lead_out[AT_IDS + 16 : SENT_LEAD, :] = jnp.concatenate([middle, low], axis=0).astype(BF)


def upper(size):
    row = lax.broadcasted_iota(jnp.int32, (size, size), 0)
    col = lax.broadcasted_iota(jnp.int32, (size, size), 1)
    return (row <= col).astype(F32).astype(BF)


def place_rows():
    return (lax.broadcasted_iota(jnp.int32, (SLOTS, GTOK), 0) + 1).astype(F32)


def pick_rows(rank, group, pick_s):
    place = place_rows()
    for e in range(LO):
        picks = rank[group * LO + e : group * LO + e + 1, :] == place
        pick_s[e * SLOTS : (e + 1) * SLOTS, :] = jnp.where(picks, 1.0, 0.0).astype(BF)


def put_rows(out, group, rows, lanes):
    for e in range(LO):
        to = (e * GROUPS + group) * SLOTS
        out[to : to + SLOTS, lanes] = rows[e * SLOTS : (e + 1) * SLOTS, :].astype(BF)


def first_kernel(first, got, x_out, rank_out, ids_out, gate_out, tok_s, pick_s):
    base = (first[0] * LO).astype(F32)
    upto = upper(GTOK)
    for g in range(GROUPS):
        named, weights = [], []
        for b in range(PACK):
            at = (g * PACK + b) * SENT_LEAD
            for f in range(FIRST):
                cut = slice(f * LANES, (f + 1) * LANES)
                tok_s[b * TOK : (b + 1) * TOK, cut] = got[at + f * TOK : at + (f + 1) * TOK, :]
            one = got[at + AT_IDS : at + AT_IDS + 16, :].astype(F32)
            two = got[at + AT_IDS + 16 : at + SENT_LEAD, :].astype(F32)
            named.append(one[:TOP])
            weights.append((one[TOP:] + two[:TOP]) + two[TOP:])
        ids = jnp.concatenate(named, axis=1)
        weights = jnp.concatenate(weights, axis=1)
        ids_out[g * TOP : (g + 1) * TOP, :] = ids
        named, weight = [], []
        for e in range(LO):
            same = ids == base + e
            named.append(jnp.sum(jnp.where(same, 1.0, 0.0), axis=0, keepdims=True))
            weight.append(jnp.sum(jnp.where(same, weights, 0.0), axis=0, keepdims=True))
        named = jnp.concatenate(named, axis=0)
        gate_out[g * LO : (g + 1) * LO, :] = jnp.concatenate(weight, axis=0)
        rank_out[g * LO : (g + 1) * LO, :] = named * nn(named.astype(BF), upto)
        pick_rows(rank_out, g, pick_s)
        put_rows(x_out, g, nn(pick_s[...], tok_s[...]), slice(0, LEAD))


def cotangents(got, group, kept):
    for b in range(PACK):
        at = (group * PACK + b) * SENT_REST + AT_COT
        for f in range(CUTS):
            cut = slice(f * LANES, (f + 1) * LANES)
            kept[b * TOK : (b + 1) * TOK, cut] = got[at + f * TOK : at + (f + 1) * TOK, :]


def rest_kernel(lead, got, rank, gate, out, late_out, tok_s, cot_s, pick_s):
    for g in range(GROUPS):
        cotangents(got, g, cot_s)
        for b in range(PACK):
            at = (g * PACK + b) * SENT_LEAD
            tok_s[b * TOK : b * TOK + PART, :] = lead[at + LEAD : at + AT_IDS, :]
            at = (g * PACK + b) * SENT_REST
            tok_s[b * TOK + PART : (b + 1) * TOK, :] = got[at : at + AT_COT, :]
        pick_rows(rank, g, pick_s)
        scale = []
        for e in range(LO):
            picked = pick_s[e * SLOTS : (e + 1) * SLOTS, :].astype(F32)
            weight = gate[g * LO + e : g * LO + e + 1, :]
            scale.append(jnp.sum(picked * weight, axis=1, keepdims=True))
        put_rows(out, g, nn(pick_s[...], tok_s[...]), slice(0, TAIL))
        grads = jnp.concatenate(scale, axis=0) * nn(pick_s[...], cot_s[...])
        put_rows(out, g, grads[:, :EARLY], slice(TAIL, MIXED))
        put_rows(late_out, g, grads[:, EARLY:], slice(0, WIDTH - EARLY))


TILE = 160


def tiles(step):
    def one(i, carry):
        step(pl.ds(pl.multiple_of(i * TILE, 16), TILE))
        return carry

    lax.fori_loop(0, ROWS // TILE, one, 0)


def gated(x, rest, w_gate, w_up, rows):
    tok = jnp.concatenate([x[rows, :], rest[rows, :TAIL]], axis=1)
    gate_pre = nn(tok, w_gate[...])
    up_pre = nn(tok, w_up[...])
    sig = jax.nn.sigmoid(gate_pre)
    activation = gate_pre * sig
    hidden = (activation * up_pre).astype(BF)
    return gate_pre, up_pre, sig, activation, hidden


def forward_kernel(x, rest, w_gate, w_up, w_down, out):
    def step(rows):
        hidden = gated(x, rest, w_gate, w_up, rows)[-1]
        out[rows, :] = nn(hidden, w_down[...]).astype(BF)

    tiles(step)


def backward_kernel(x, rest, late, w_gate, w_up, w_down, out, weight, hidden_s, gate_s, up_s):
    def step(rows):
        gate_pre, up_pre, sig, activation, hidden = gated(x, rest, w_gate, w_up, rows)
        grads = jnp.concatenate([rest[rows, TAIL:], late[rows, :]], axis=1)
        hidden_grad = nt(grads, w_down[...])
        slope = sig * (1.0 + gate_pre * (1.0 - sig))
        gate = (hidden_grad * up_pre * slope).astype(BF)
        up = (hidden_grad * activation).astype(BF)
        hidden_s[rows, :] = hidden
        gate_s[rows, :] = gate
        up_s[rows, :] = up
        out[rows, :] = (nt(gate, w_gate[...]) + nt(up, w_up[...])).astype(BF)

    tiles(step)
    for n, side in enumerate((gate_s, up_s)):
        at = n * WIDTH
        weight[at : at + LEAD, :] = tn(x[...], side[...]).astype(BF)
        weight[at + LEAD : at + WIDTH, :] = tn(rest[:, :TAIL], side[...]).astype(BF)
    weight[2 * WIDTH :, :EARLY] = tn(hidden_s[...], rest[:, TAIL:]).astype(BF)
    weight[2 * WIDTH :, EARLY:] = tn(hidden_s[...], late[...]).astype(BF)


def split(value):
    high = value.astype(BF)
    return high, (value - high.astype(F32)).astype(BF)


def layer_kernel(first, got, rank, ids, gate, eo, out, picks_out, cot_s, eo_s):
    base = (first[0] * LO).astype(F32)
    expert = lax.broadcasted_iota(jnp.int32, (LO, ALL), 0)
    slot = lax.broadcasted_iota(jnp.int32, (LO, ALL), 1)
    spread = ((slot >= expert * SLOTS) & (slot < (expert + 1) * SLOTS)).astype(F32).astype(BF)
    lane = lax.broadcasted_iota(jnp.int32, (1, ALL), 1)
    place = (lane - SLOTS * lax.div(lane, SLOTS) + 1).astype(F32)
    for g in range(GROUPS):
        cotangents(got, g, cot_s)
        for e in range(LO):
            at = (e * GROUPS + g) * SLOTS
            eo_s[e * SLOTS : (e + 1) * SLOTS, :] = eo[at : at + SLOTS, :]
        rows = slice(g * LO, (g + 1) * LO)
        picks = tn(rank[rows, :].astype(BF), spread) == place
        picks_out[g * GTOK : (g + 1) * GTOK, :] = jnp.where(picks, 1.0, 0.0).astype(BF)
        high, low = split(gate[rows, :])
        high = jnp.where(picks, tn(high, spread), 0.0).astype(BF)
        low = jnp.where(picks, tn(low, spread), 0.0).astype(BF)
        layer = nn(high, eo_s[...]) + nn(low, eo_s[...])
        along = jnp.where(picks, nt(cot_s[...], eo_s[...]), 0.0)
        high, low = split(along)
        along = nt(spread, high) + nt(spread, low)
        named = ids[g * TOP : (g + 1) * TOP, :]
        grad = jnp.zeros((TOP, GTOK), F32)
        for e in range(LO):
            grad += jnp.where(named == base + e, along[e : e + 1, :], 0.0)
        grad_high = grad.astype(BF).astype(F32)
        grad = jnp.concatenate([grad_high, grad - grad_high], axis=0).astype(BF)
        for b in range(PACK):
            at = g * PACK + b
            for f in range(CUTS):
                here = layer[b * TOK : (b + 1) * TOK, f * LANES : (f + 1) * LANES]
                out[at, f * TOK : (f + 1) * TOK, :] = here.astype(BF)
            out[at, 2 * WIDTH : BACK, :] = grad[:, b * TOK : (b + 1) * TOK]


def back_kernel(picks, ib, held, out, ib_s, sent_s, sems):
    del held
    copies = []
    for g in range(GROUPS):
        for e in range(LO):
            at = (e * GROUPS + g) * SLOTS
            ib_s[e * SLOTS : (e + 1) * SLOTS, :] = ib[at : at + SLOTS, :]
        back = nn(picks[g * GTOK : (g + 1) * GTOK, :], ib_s[...])
        for b in range(PACK):
            n = g * PACK + b
            for f in range(CUTS):
                here = back[b * TOK : (b + 1) * TOK, f * LANES : (f + 1) * LANES]
                sent_s[n, f * TOK : (f + 1) * TOK, :] = here.astype(BF)
            copy = pltpu.make_async_copy(
                sent_s.at[n],
                out.at[n, pl.ds(WIDTH, WIDTH), :],
                sems.at[n],
            )
            copy.start()
            copies.append(copy)
    for copy in copies:
        copy.wait()


def unpack_kernel(got, layer, back, grad):
    for f in range(CUTS):
        cut = slice(f * LANES, (f + 1) * LANES)
        layer[:, cut] = got[f * TOK : (f + 1) * TOK, :]
        back[:, cut] = got[WIDTH + f * TOK : WIDTH + (f + 1) * TOK, :]
    parts = got[2 * WIDTH : BACK, :].astype(F32)
    grad[...] = parts[:TOP] + parts[TOP:]


def body(tokens, expert_ids, gate_weights, cotangent, w_gate, w_up, w_down):
    shape = jax.ShapeDtypeStruct
    first = lax.axis_index("hi").astype(jnp.int32).reshape(1)
    w_gate, w_up, w_down = w_gate[0], w_up[0], w_down[0]
    square = 2 * ROWS * WIDTH * WIDTH
    lead_sent, rest_sent = call(
        pack_kernel,
        [shape((SENT_LEAD, LANES), BF), shape((SENT_REST, LANES), BF)],
        [tokens, expert_ids.T, gate_weights.T, cotangent],
        room=56,
    )
    got = lax.all_gather(rest_sent, "hi", axis=0, tiled=True)
    lead = lax.all_gather(lead_sent, "hi", axis=0, tiled=True)
    picked = pltpu.VMEM((ALL, GTOK), BF)
    small = shape((GROUPS * LO, GTOK), F32)
    rows_first, rank, ids, gate = call(
        first_kernel,
        [shape((ROWS, LEAD), BF), small, shape((GROUPS * TOP, GTOK), F32), small],
        [first, lead],
        [pltpu.VMEM((GTOK, LEAD), BF), picked],
        scalars=1,
    )
    rows_rest, rows_late = call(
        rest_kernel,
        [shape((ROWS, MIXED), BF), shape((ROWS, WIDTH - EARLY), BF)],
        [lead, got, rank, gate],
        [pltpu.VMEM((GTOK, TAIL), BF), pltpu.VMEM((GTOK, WIDTH), BF), picked],
        flops=100 * square,
        room=ROOM,
    )
    exchange = functools.partial(
        lax.all_to_all, axis_name="lo", split_axis=0, concat_axis=0, tiled=True
    )
    x = exchange(rows_first)
    rest = exchange(rows_rest)
    late = exchange(rows_late)
    narrow = shape((ROWS, WIDTH), BF)
    (expert_out,) = call(
        forward_kernel, [narrow], [x, rest, w_gate, w_up, w_down], flops=3 * square
    )
    eo = exchange(expert_out)
    whole = pltpu.VMEM((ROWS, WIDTH), BF)
    input_back, weight_part = call(
        backward_kernel,
        [narrow, shape((3 * WIDTH, WIDTH), BF)],
        [x, rest, late, w_gate, w_up, w_down],
        [whole, whole, whole],
        flops=8 * square,
        room=56,
    )
    eo, input_back = lax.optimization_barrier((eo, input_back))
    ib = exchange(input_back)
    partial, picks = call(
        layer_kernel,
        [shape((HI, BACK, LANES), BF), shape((GROUPS * GTOK, ALL), BF)],
        [first, got, rank, ids, gate, eo],
        [pltpu.VMEM((GTOK, WIDTH), BF), pltpu.VMEM((ALL, WIDTH), BF)],
        scalars=1,
        room=ROOM,
        flops=3 * square,
    )
    partial = pl.pallas_call(
        back_kernel,
        out_shape=shape((HI, BACK, LANES), BF),
        in_specs=[VMEM, VMEM, pl.BlockSpec(memory_space=pl.ANY)],
        out_specs=pl.BlockSpec(memory_space=pl.ANY),
        scratch_shapes=[
            pltpu.VMEM((ALL, WIDTH), BF),
            pltpu.VMEM((HI, WIDTH, LANES), BF),
            pltpu.SemaphoreType.DMA((HI,)),
        ],
        input_output_aliases={2: 0},
        compiler_params=pltpu.CompilerParams(vmem_limit_bytes=24 * MIB),
        cost_estimate=pl.CostEstimate(flops=square, bytes_accessed=4 << 20, transcendentals=0),
    )(picks, ib, partial)
    summed = lax.psum_scatter(
        partial.reshape(HI * BACK, LANES), "hi", scatter_dimension=0, tiled=True
    )
    over_dp = functools.partial(
        lax.all_to_all, axis_name="dp", split_axis=0, concat_axis=0, tiled=True
    )
    data = lax.axis_size("dp")
    share = over_dp(weight_part).reshape(data, -1, WIDTH).astype(F32)
    grad_scale = float(data * TOK * TOP) ** (-0.5)
    share = (jnp.sum(share, axis=0) * grad_scale).astype(BF)
    weight_grad = over_dp(jnp.tile(share, (data, 1))).reshape(3, 1, WIDTH, WIDTH)
    layer_out, grad_tokens, grad_gates = call(
        unpack_kernel,
        [shape((TOK, WIDTH), BF), shape((TOK, WIDTH), BF), shape((TOP, LANES), F32)],
        [summed],
        room=56,
    )
    return (
        layer_out,
        grad_tokens,
        grad_gates.T,
        weight_grad[0],
        weight_grad[1],
        weight_grad[2],
    )


def solution(mesh):
    data = mesh.shape["dp"]
    cut = Mesh(mesh.devices.reshape(data, HI, LO), ("dp", "hi", "lo"))
    rows = P(("dp", "hi", "lo"), None)
    weight = P(("hi", "lo"), None, None)
    return jax.shard_map(
        body,
        mesh=cut,
        in_specs=(rows, rows, rows, rows, weight, weight, weight),
        out_specs=(rows, rows, rows, weight, weight, weight),
        check_vma=False,
    )
```

```python
import functools
import jax
import jax.numpy as jnp
from jax import lax
from jax.experimental import pallas as pl
from jax.experimental.pallas import tpu as pltpu
from jax.sharding import Mesh, PartitionSpec as P

BF = jnp.bfloat16
F32 = jnp.float32
TOK = 128
WIDTH = 512
TOP = 8
CAP = 20
HI = 8
LO = 8
PACK = 4
GROUPS = HI // PACK
SLOTS = PACK * CAP
GTOK = PACK * TOK
LANES = 128
CUTS = WIDTH // LANES
FIRST = 3
SECOND = CUTS - FIRST
LEAD = FIRST * LANES
TAIL = SECOND * LANES
PART = TOK // 2
AT_IDS = LEAD + PART
SENT_LEAD = AT_IDS + 4 * TOP
SENT_REST = TOK - PART + WIDTH
EARLY = 256
MIXED = TAIL + EARLY
AT_COT = TOK - PART
BACK = 2 * WIDTH + 2 * TOP
ALL = LO * SLOTS
ROWS = HI * CAP * LO
MIB = 1024 * 1024
ROOM = 24
VMEM = pl.BlockSpec(memory_space=pltpu.VMEM)
SMEM = pl.BlockSpec(memory_space=pltpu.SMEM)


def nn(a, b):
    return jnp.dot(a, b, preferred_element_type=F32)


def nt(a, b):
    return lax.dot_general(a, b, (((1,), (1,)), ((), ())), preferred_element_type=F32)


def tn(a, b):
    return lax.dot_general(a, b, (((0,), (0,)), ((), ())), preferred_element_type=F32)


def call(kernel, shapes, args, scratch=(), scalars=0, flops=0, room=24):
    moved = sum(a.size * a.dtype.itemsize for a in args)
    moved += sum(s.size * s.dtype.itemsize for s in shapes)
    return pl.pallas_call(
        kernel,
        out_shape=shapes,
        in_specs=[SMEM] * scalars + [VMEM] * (len(args) - scalars),
        out_specs=[VMEM] * len(shapes),
        scratch_shapes=list(scratch),
        compiler_params=pltpu.CompilerParams(vmem_limit_bytes=room * MIB),
        cost_estimate=pl.CostEstimate(flops=flops, bytes_accessed=moved, transcendentals=0),
    )(*args)


def pack_kernel(tok, ids, gates, cot, lead_out, rest_out):
    for f in range(CUTS):
        cut = slice(f * LANES, (f + 1) * LANES)
        if f < FIRST:
            lead_out[f * TOK : (f + 1) * TOK, :] = tok[:, cut]
        rest_out[AT_COT + f * TOK : AT_COT + (f + 1) * TOK, :] = cot[:, cut]
    lead_out[LEAD:AT_IDS, :] = tok[:PART, LEAD:]
    rest_out[:AT_COT, :] = tok[PART:, LEAD:]
    gate = gates[...]
    high = gate.astype(BF).astype(F32)
    middle = (gate - high).astype(BF).astype(F32)
    low = gate - high - middle
    named = ids[...].astype(F32)
    lead_out[AT_IDS : AT_IDS + 16, :] = jnp.concatenate([named, high], axis=0).astype(BF)
    lead_out[AT_IDS + 16 : SENT_LEAD, :] = jnp.concatenate([middle, low], axis=0).astype(BF)


def upper(size):
    row = lax.broadcasted_iota(jnp.int32, (size, size), 0)
    col = lax.broadcasted_iota(jnp.int32, (size, size), 1)
    return (row <= col).astype(F32).astype(BF)


def place_rows():
    return (lax.broadcasted_iota(jnp.int32, (SLOTS, GTOK), 0) + 1).astype(F32)


def pick_rows(rank, group, pick_s):
    place = place_rows()
    for e in range(LO):
        picks = rank[group * LO + e : group * LO + e + 1, :] == place
        pick_s[e * SLOTS : (e + 1) * SLOTS, :] = jnp.where(picks, 1.0, 0.0).astype(BF)


def put_rows(out, group, rows, lanes):
    for e in range(LO):
        to = (e * GROUPS + group) * SLOTS
        out[to : to + SLOTS, lanes] = rows[e * SLOTS : (e + 1) * SLOTS, :].astype(BF)


def first_kernel(first, got, x_out, rank_out, ids_out, gate_out, tok_s, pick_s):
    base = (first[0] * LO).astype(F32)
    upto = upper(GTOK)
    for g in range(GROUPS):
        named, weights = [], []
        for b in range(PACK):
            at = (g * PACK + b) * SENT_LEAD
            for f in range(FIRST):
                cut = slice(f * LANES, (f + 1) * LANES)
                tok_s[b * TOK : (b + 1) * TOK, cut] = got[at + f * TOK : at + (f + 1) * TOK, :]
            one = got[at + AT_IDS : at + AT_IDS + 16, :].astype(F32)
            two = got[at + AT_IDS + 16 : at + SENT_LEAD, :].astype(F32)
            named.append(one[:TOP])
            weights.append((one[TOP:] + two[:TOP]) + two[TOP:])
        ids = jnp.concatenate(named, axis=1)
        weights = jnp.concatenate(weights, axis=1)
        ids_out[g * TOP : (g + 1) * TOP, :] = ids
        named, weight = [], []
        for e in range(LO):
            same = ids == base + e
            named.append(jnp.sum(jnp.where(same, 1.0, 0.0), axis=0, keepdims=True))
            weight.append(jnp.sum(jnp.where(same, weights, 0.0), axis=0, keepdims=True))
        named = jnp.concatenate(named, axis=0)
        gate_out[g * LO : (g + 1) * LO, :] = jnp.concatenate(weight, axis=0)
        rank_out[g * LO : (g + 1) * LO, :] = named * nn(named.astype(BF), upto)
        pick_rows(rank_out, g, pick_s)
        put_rows(x_out, g, nn(pick_s[...], tok_s[...]), slice(0, LEAD))


def cotangents(got, group, kept):
    for b in range(PACK):
        at = (group * PACK + b) * SENT_REST + AT_COT
        for f in range(CUTS):
            cut = slice(f * LANES, (f + 1) * LANES)
            kept[b * TOK : (b + 1) * TOK, cut] = got[at + f * TOK : at + (f + 1) * TOK, :]


def rest_kernel(lead, got, rank, gate, out, late_out, tok_s, cot_s, pick_s):
    for g in range(GROUPS):
        cotangents(got, g, cot_s)
        for b in range(PACK):
            at = (g * PACK + b) * SENT_LEAD
            tok_s[b * TOK : b * TOK + PART, :] = lead[at + LEAD : at + AT_IDS, :]
            at = (g * PACK + b) * SENT_REST
            tok_s[b * TOK + PART : (b + 1) * TOK, :] = got[at : at + AT_COT, :]
        pick_rows(rank, g, pick_s)
        scale = []
        for e in range(LO):
            picked = pick_s[e * SLOTS : (e + 1) * SLOTS, :].astype(F32)
            weight = gate[g * LO + e : g * LO + e + 1, :]
            scale.append(jnp.sum(picked * weight, axis=1, keepdims=True))
        put_rows(out, g, nn(pick_s[...], tok_s[...]), slice(0, TAIL))
        grads = jnp.concatenate(scale, axis=0) * nn(pick_s[...], cot_s[...])
        put_rows(out, g, grads[:, :EARLY], slice(TAIL, MIXED))
        put_rows(late_out, g, grads[:, EARLY:], slice(0, WIDTH - EARLY))


TILE = 160


def tiles(step):
    def one(i, carry):
        step(pl.ds(pl.multiple_of(i * TILE, 16), TILE))
        return carry

    lax.fori_loop(0, ROWS // TILE, one, 0)


def gated(x, rest, w_gate, w_up, rows):
    tok = jnp.concatenate([x[rows, :], rest[rows, :TAIL]], axis=1)
    gate_pre = nn(tok, w_gate[...])
    up_pre = nn(tok, w_up[...])
    sig = jax.nn.sigmoid(gate_pre)
    activation = gate_pre * sig
    hidden = (activation * up_pre).astype(BF)
    return gate_pre, up_pre, sig, activation, hidden


def forward_kernel(x, rest, w_gate, w_up, w_down, out):
    def step(rows):
        hidden = gated(x, rest, w_gate, w_up, rows)[-1]
        out[rows, :] = nn(hidden, w_down[...]).astype(BF)

    tiles(step)


def backward_kernel(x, rest, late, w_gate, w_up, w_down, out, weight, hidden_s, gate_s, up_s):
    def step(rows):
        gate_pre, up_pre, sig, activation, hidden = gated(x, rest, w_gate, w_up, rows)
        grads = jnp.concatenate([rest[rows, TAIL:], late[rows, :]], axis=1)
        hidden_grad = nt(grads, w_down[...])
        slope = sig * (1.0 + gate_pre * (1.0 - sig))
        gate = (hidden_grad * up_pre * slope).astype(BF)
        up = (hidden_grad * activation).astype(BF)
        hidden_s[rows, :] = hidden
        gate_s[rows, :] = gate
        up_s[rows, :] = up
        out[rows, :] = (nt(gate, w_gate[...]) + nt(up, w_up[...])).astype(BF)

    tiles(step)
    for n, side in enumerate((gate_s, up_s)):
        at = n * WIDTH
        weight[at : at + LEAD, :] = tn(x[...], side[...]).astype(BF)
        weight[at + LEAD : at + WIDTH, :] = tn(rest[:, :TAIL], side[...]).astype(BF)
    weight[2 * WIDTH :, :EARLY] = tn(hidden_s[...], rest[:, TAIL:]).astype(BF)
    weight[2 * WIDTH :, EARLY:] = tn(hidden_s[...], late[...]).astype(BF)


def split(value):
    high = value.astype(BF)
    return high, (value - high.astype(F32)).astype(BF)


def layer_kernel(first, got, rank, ids, gate, eo, out, picks_out, cot_s, eo_s):
    base = (first[0] * LO).astype(F32)
    expert = lax.broadcasted_iota(jnp.int32, (LO, ALL), 0)
    slot = lax.broadcasted_iota(jnp.int32, (LO, ALL), 1)
    spread = ((slot >= expert * SLOTS) & (slot < (expert + 1) * SLOTS)).astype(F32).astype(BF)
    lane = lax.broadcasted_iota(jnp.int32, (1, ALL), 1)
    place = (lane - SLOTS * lax.div(lane, SLOTS) + 1).astype(F32)
    for g in range(GROUPS):
        cotangents(got, g, cot_s)
        for e in range(LO):
            at = (e * GROUPS + g) * SLOTS
            eo_s[e * SLOTS : (e + 1) * SLOTS, :] = eo[at : at + SLOTS, :]
        rows = slice(g * LO, (g + 1) * LO)
        picks = tn(rank[rows, :].astype(BF), spread) == place
        picks_out[g * GTOK : (g + 1) * GTOK, :] = jnp.where(picks, 1.0, 0.0).astype(BF)
        high, low = split(gate[rows, :])
        high = jnp.where(picks, tn(high, spread), 0.0).astype(BF)
        low = jnp.where(picks, tn(low, spread), 0.0).astype(BF)
        layer = nn(high, eo_s[...]) + nn(low, eo_s[...])
        along = jnp.where(picks, nt(cot_s[...], eo_s[...]), 0.0)
        high, low = split(along)
        along = nt(spread, high) + nt(spread, low)
        named = ids[g * TOP : (g + 1) * TOP, :]
        grad = jnp.zeros((TOP, GTOK), F32)
        for e in range(LO):
            grad += jnp.where(named == base + e, along[e : e + 1, :], 0.0)
        grad_high = grad.astype(BF).astype(F32)
        grad = jnp.concatenate([grad_high, grad - grad_high], axis=0).astype(BF)
        for b in range(PACK):
            at = g * PACK + b
            for f in range(CUTS):
                here = layer[b * TOK : (b + 1) * TOK, f * LANES : (f + 1) * LANES]
                out[at, f * TOK : (f + 1) * TOK, :] = here.astype(BF)
            out[at, 2 * WIDTH : BACK, :] = grad[:, b * TOK : (b + 1) * TOK]


def back_kernel(picks, ib, held, out, ib_s, sent_s, sems):
    del held
    copies = []
    for g in range(GROUPS):
        for e in range(LO):
            at = (e * GROUPS + g) * SLOTS
            ib_s[e * SLOTS : (e + 1) * SLOTS, :] = ib[at : at + SLOTS, :]
        back = nn(picks[g * GTOK : (g + 1) * GTOK, :], ib_s[...])
        for b in range(PACK):
            n = g * PACK + b
            for f in range(CUTS):
                here = back[b * TOK : (b + 1) * TOK, f * LANES : (f + 1) * LANES]
                sent_s[n, f * TOK : (f + 1) * TOK, :] = here.astype(BF)
            copy = pltpu.make_async_copy(
                sent_s.at[n],
                out.at[n, pl.ds(WIDTH, WIDTH), :],
                sems.at[n],
            )
            copy.start()
            copies.append(copy)
    for copy in copies:
        copy.wait()


def unpack_kernel(got, layer, back, grad):
    for f in range(CUTS):
        cut = slice(f * LANES, (f + 1) * LANES)
        layer[:, cut] = got[f * TOK : (f + 1) * TOK, :]
        back[:, cut] = got[WIDTH + f * TOK : WIDTH + (f + 1) * TOK, :]
    parts = got[2 * WIDTH : BACK, :].astype(F32)
    grad[...] = parts[:TOP] + parts[TOP:]


def body(tokens, expert_ids, gate_weights, cotangent, w_gate, w_up, w_down):
    shape = jax.ShapeDtypeStruct
    first = lax.axis_index("hi").astype(jnp.int32).reshape(1)
    w_gate, w_up, w_down = w_gate[0], w_up[0], w_down[0]
    square = 2 * ROWS * WIDTH * WIDTH
    lead_sent, rest_sent = call(
        pack_kernel,
        [shape((SENT_LEAD, LANES), BF), shape((SENT_REST, LANES), BF)],
        [tokens, expert_ids.T, gate_weights.T, cotangent],
        room=56,
    )
    got = lax.all_gather(rest_sent, "hi", axis=0, tiled=True)
    lead = lax.all_gather(lead_sent, "hi", axis=0, tiled=True)
    picked = pltpu.VMEM((ALL, GTOK), BF)
    small = shape((GROUPS * LO, GTOK), F32)
    rows_first, rank, ids, gate = call(
        first_kernel,
        [shape((ROWS, LEAD), BF), small, shape((GROUPS * TOP, GTOK), F32), small],
        [first, lead],
        [pltpu.VMEM((GTOK, LEAD), BF), picked],
        scalars=1,
    )
    rows_rest, rows_late = call(
        rest_kernel,
        [shape((ROWS, MIXED), BF), shape((ROWS, WIDTH - EARLY), BF)],
        [lead, got, rank, gate],
        [pltpu.VMEM((GTOK, TAIL), BF), pltpu.VMEM((GTOK, WIDTH), BF), picked],
        flops=100 * square,
        room=56,
    )
    exchange = functools.partial(
        lax.all_to_all, axis_name="lo", split_axis=0, concat_axis=0, tiled=True
    )
    x = exchange(rows_first)
    rest = exchange(rows_rest)
    late = exchange(rows_late)
    narrow = shape((ROWS, WIDTH), BF)
    (expert_out,) = call(
        forward_kernel, [narrow], [x, rest, w_gate, w_up, w_down], flops=3 * square
    )
    eo = exchange(expert_out)
    whole = pltpu.VMEM((ROWS, WIDTH), BF)
    input_back, weight_part = call(
        backward_kernel,
        [narrow, shape((3 * WIDTH, WIDTH), BF)],
        [x, rest, late, w_gate, w_up, w_down],
        [whole, whole, whole],
        flops=8 * square,
        room=56,
    )
    eo, input_back = lax.optimization_barrier((eo, input_back))
    ib = exchange(input_back)
    partial, picks = call(
        layer_kernel,
        [shape((HI, BACK, LANES), BF), shape((GROUPS * GTOK, ALL), BF)],
        [first, got, rank, ids, gate, eo],
        [pltpu.VMEM((GTOK, WIDTH), BF), pltpu.VMEM((ALL, WIDTH), BF)],
        scalars=1,
        room=ROOM,
        flops=3 * square,
    )
    partial = pl.pallas_call(
        back_kernel,
        out_shape=shape((HI, BACK, LANES), BF),
        in_specs=[VMEM, VMEM, pl.BlockSpec(memory_space=pl.ANY)],
        out_specs=pl.BlockSpec(memory_space=pl.ANY),
        scratch_shapes=[
            pltpu.VMEM((ALL, WIDTH), BF),
            pltpu.VMEM((HI, WIDTH, LANES), BF),
            pltpu.SemaphoreType.DMA((HI,)),
        ],
        input_output_aliases={2: 0},
        compiler_params=pltpu.CompilerParams(vmem_limit_bytes=24 * MIB),
        cost_estimate=pl.CostEstimate(flops=square, bytes_accessed=4 << 20, transcendentals=0),
    )(picks, ib, partial)
    summed = lax.psum_scatter(
        partial.reshape(HI * BACK, LANES), "hi", scatter_dimension=0, tiled=True
    )
    over_dp = functools.partial(
        lax.all_to_all, axis_name="dp", split_axis=0, concat_axis=0, tiled=True
    )
    data = lax.axis_size("dp")
    share = over_dp(weight_part).reshape(data, -1, WIDTH).astype(F32)
    grad_scale = float(data * TOK * TOP) ** (-0.5)
    share = (jnp.sum(share, axis=0) * grad_scale).astype(BF)
    weight_grad = over_dp(jnp.tile(share, (data, 1))).reshape(3, 1, WIDTH, WIDTH)
    layer_out, grad_tokens, grad_gates = call(
        unpack_kernel,
        [shape((TOK, WIDTH), BF), shape((TOK, WIDTH), BF), shape((TOP, LANES), F32)],
        [summed],
        room=56,
    )
    return (
        layer_out,
        grad_tokens,
        grad_gates.T,
        weight_grad[0],
        weight_grad[1],
        weight_grad[2],
    )


def solution(mesh):
    data = mesh.shape["dp"]
    cut = Mesh(mesh.devices.reshape(data, HI, LO), ("dp", "hi", "lo"))
    rows = P(("dp", "hi", "lo"), None)
    weight = P(("hi", "lo"), None, None)
    return jax.shard_map(
        body,
        mesh=cut,
        in_specs=(rows, rows, rows, rows, weight, weight, weight),
        out_specs=(rows, rows, rows, weight, weight, weight),
        check_vma=False,
    )
```
